256 devices in a mesh: batch: 16 (over z, y_lo), row: 16 (over x, y_hi, core).
Axes of the slice: x: 4, y: 4 (y_hi: 2, y_lo: 2; y = y_hi * 2 + y_lo), z: 8, core: 2. Of those that a mesh axis runs over, the one named last changes fastest.
Arguments:
- probe_real: float32 [2048, 2048], P('row'), may hold values from -6 to 6
- probe_imag: float32 [2048, 2048], P('row'), may hold values from -6 to 6
- object_real: float32 [2048, 2304], P('row'), may hold values from -5 to 5
- object_imag: float32 [2048, 2304], P('row'), may hold values from -5 to 5
- amplitudes: float32 [16, 2048, 2048], P('batch', 'row'), may hold values from 0.2 to 3
- row_shift: int32 [16], P('batch'), may hold values from 0 to 127
- col_shift: int32 [16], P('batch'), may hold values from 0 to 256
Outputs:
- probe_grad_real: float32 [2048, 2048], P('row', 'batch')
- probe_grad_imag: float32 [2048, 2048], P('row', 'batch')
- object_grad_real: float32 [2048, 2304], P('row', 'batch')
- object_grad_imag: float32 [2048, 2304], P('row', 'batch')
The draws below stay inside these ranges and needn't reach their ends.
All inputs are finite; a program needn't handle non-finite values.
Results may differ from the reference program's by a relative error of at most 0.0003.
Values sent between devices are 32-bit elements; how exact they have to be, the bound alone decides.
No kernel may reach another device: no remote copies, remote signals or barrier semaphores. Data moves between devices by JAX's collectives and lax.ppermute only.
A program may use at most 128 MiB of HBM per device.

```python
import math
import jax
import jax.numpy as jnp
from jax import lax

M = 2048
SPAN = 256
P_SIZE = 16
OC = 2304
N_ROW = 16


def plant(array, rng, smallest, largest):
    extent = array.shape
    index_at = [jax.random.randint(jax.random.fold_in(rng, axis), (), 0, extent[axis]) for axis in range(len(extent))]
    array = array.at[tuple(index_at)].set(smallest)
    longest = extent.index(max(extent))
    index_at[longest] = (index_at[longest] + 1) % extent[longest]
    return array.at[tuple(index_at)].set(largest)


def block_scale(own_key, shape, shards, low, high):
    gain = 1.0
    for dim, blocks in shards:
        draws = jax.random.uniform(jax.random.fold_in(jax.random.fold_in(own_key, 6), dim), (blocks,), jnp.float32, low / len(shards), high / len(shards))
        gain = gain * jnp.repeat(jnp.exp(draws), shape[dim] // blocks).reshape((-1,) + (1,) * (len(shape) - 1 - dim))
    return gain


def normal_values(own_key, extent, spread, limit, cuts=(), kind=jnp.bfloat16):
    factor_of = block_scale(own_key, extent, cuts, -0.22, 0.18) if cuts else 1.0
    entries = jax.random.normal(own_key, extent, jnp.float32) * spread * factor_of
    return jnp.minimum(jnp.maximum(entries, -limit), limit).astype(kind)


def setup_inputs(seed: int = 0) -> dict:
    key_list = jax.random.split(jax.random.key(seed), 8)
    probe_real = normal_values(key_list[0], (M, M), 1.0, 6.0, ((0, 16),), jnp.float32)
    probe_imag = normal_values(key_list[1], (M, M), 1.0, 6.0, ((0, 16),), jnp.float32)
    object_real = normal_values(key_list[2], (M, OC), 0.7, 5.0, ((0, 16),), jnp.float32)
    object_imag = normal_values(key_list[3], (M, OC), 0.7, 5.0, ((0, 16),), jnp.float32)
    amplitudes = jnp.clip(jnp.exp(math.log(3.0) - 2.7080502 * jax.random.uniform(key_list[4], (P_SIZE, M, M), jnp.float32) ** block_scale(key_list[4], (P_SIZE, M, M), ((0, 16), (1, 16)), -0.2, 0.2)), 0.2, 3.0)
    row_shift = plant(jax.random.randint(key_list[5], (P_SIZE,), 0, M // N_ROW), jax.random.fold_in(key_list[5], 1), 0, (M // N_ROW) - 1).astype(jnp.int32)
    col_shift = plant(jax.random.randint(key_list[6], (P_SIZE,), 0, SPAN + 1), jax.random.fold_in(key_list[6], 1), 0, SPAN).astype(jnp.int32)
    return dict(probe_real=probe_real, probe_imag=probe_imag, object_real=object_real, object_imag=object_imag, amplitudes=amplitudes, row_shift=row_shift, col_shift=col_shift)


def chirp(length, direction):
    indices = jnp.arange(length, dtype=jnp.int32)
    frequency = jnp.where(indices < length // 2, indices, indices - length)
    turn_count = (frequency * frequency) % (4 * length)
    angles = (direction * 2.0 * math.pi / (4 * length)) * turn_count.astype(jnp.float32)
    return jnp.cos(angles) + 1j * jnp.sin(angles)


def propagate(wave_field, transfer):
    wave_field = jnp.fft.ifft(jnp.fft.fft(wave_field, axis=1) * transfer[None, :], axis=1)
    return jnp.fft.ifft(jnp.fft.fft(wave_field, axis=0) * transfer[:, None], axis=0)


def reference(probe_real, probe_imag, object_real, object_imag, amplitudes, row_shift, col_shift):
    probe_field = probe_real + 1j * probe_imag
    object_field = object_real + 1j * object_imag
    forward_chirp = chirp(M, -1.0)
    backward_chirp = chirp(M, 1.0)

    def one_position(carry, inputs):
        probe_acc, object_acc = carry
        measured, shift_row, shift_col = inputs
        rolled = jnp.roll(object_field, -shift_row, axis=0)
        patch_field = lax.dynamic_slice_in_dim(rolled, shift_col, M, axis=1)
        wave_out = propagate(probe_field * patch_field, forward_chirp)
        magnitude = jnp.abs(wave_out)
        residual_wave = wave_out * (1.0 - measured / jnp.maximum(magnitude, 0.25))
        back_wave = propagate(residual_wave, backward_chirp)
        probe_acc = probe_acc + jnp.conj(patch_field) * back_wave
        placed = lax.dynamic_update_slice(jnp.zeros_like(object_field), jnp.conj(probe_field) * back_wave,
                                          (jnp.zeros((), jnp.int32), shift_col.astype(jnp.int32)))
        object_acc = object_acc + jnp.roll(placed, shift_row, axis=0)
        return (probe_acc, object_acc), None

    start_carry = (jnp.zeros_like(probe_field), jnp.zeros_like(object_field))
    (probe_acc, object_acc), unused = lax.scan(one_position, start_carry, (amplitudes, row_shift, col_shift))
    return (jnp.real(probe_acc).astype(jnp.float32), jnp.imag(probe_acc).astype(jnp.float32),
            jnp.real(object_acc).astype(jnp.float32), jnp.imag(object_acc).astype(jnp.float32))
```

```python
import functools
import math

import jax
import jax.numpy as jnp
import ml_dtypes
import numpy as np
from jax import lax
from jax.experimental import pallas as pl
from jax.experimental.pallas import tpu as pltpu
from jax.sharding import Mesh, PartitionSpec as P

F32 = jnp.float32
BF16 = jnp.bfloat16
LANES = 128
LEAD = 16
ROWS = 128
GROUP = 4
PART = ROWS // GROUP
VMEM_LIMIT = 56 * 1024 * 1024


def split_pair(table):
    high = table.astype(ml_dtypes.bfloat16)
    low = (table - high.astype(np.float64)).astype(ml_dtypes.bfloat16)
    return high, low


@functools.lru_cache(maxsize=None)
def propagation_tables(length):
    index = np.arange(length, dtype=np.int64)
    frequency = np.where(index < length // 2, index, index - length)
    chirp = np.exp(-2j * np.pi * ((frequency * frequency) % (4 * length)) / (4 * length))
    offsets = np.arange(-(LANES - 1), LANES, dtype=np.int64)
    place = np.arange(LANES)
    right = np.empty((LEAD, 2 * LANES, 2 * LANES))
    for c in range(LEAD):
        tone = c + LEAD * np.arange(LANES, dtype=np.int64)
        phase = np.exp(2j * np.pi * ((offsets[:, None] * tone[None, :]) % length) / length)
        line = phase @ chirp[tone] / length
        middle = line[place[:, None] - place[None, :] + LANES - 1]
        left = np.block([[middle.real, -middle.imag], [middle.imag, middle.real]])
        right[c] = left.T
    return split_pair(right) + split_pair(np.ascontiguousarray(np.swapaxes(right, 1, 2)))


def times(value, cosine, sine):
    real, imag = value
    if sine == 0.0 and cosine == 1.0:
        return value
    if cosine == 0.0 and sine == -1.0:
        return (imag, -real)
    if cosine == 0.0 and sine == 1.0:
        return (-imag, real)
    return (real * cosine - imag * sine, real * sine + imag * cosine)


def add(left, right):
    return (left[0] + right[0], left[1] + right[1])


def sub(left, right):
    return (left[0] - right[0], left[1] - right[1])


def dft4(values, sign):
    a, b, c, d = values
    even, odd = add(a, c), sub(a, c)
    both, gap = add(b, d), sub(b, d)
    turned = (-sign * gap[1], sign * gap[0]) if sign < 0 else (-gap[1], gap[0])
    if sign < 0:
        turned = (gap[1], -gap[0])
    return [add(even, both), add(odd, turned), sub(even, both), sub(odd, turned)]


def dft16(values, sign):
    inner = [dft4([values[4 * n1 + n2] for n1 in range(4)], sign) for n2 in range(4)]
    result = [None] * 16
    for k1 in range(4):
        column = []
        for n2 in range(4):
            turns = n2 * k1 % 16
            angle = 2.0 * math.pi * turns / 16
            cosine, sine = math.cos(angle), sign * math.sin(angle)
            if turns in (0, 4, 8, 12):
                cosine, sine = float(round(cosine)), float(round(sine))
            column.append(times(inner[n2][k1], cosine, sine))
        for k2, value in enumerate(dft4(column, sign)):
            result[k1 + 4 * k2] = value
    return result


def halves(value):
    high = value.astype(BF16)
    return high, (value - high.astype(F32)).astype(BF16)


def dot(left, right):
    return jnp.dot(left, right, preferred_element_type=F32)


def mix_right(store, table_high, table_low):
    rows = store.shape[1]

    def step(c, carry):
        high, low = halves(store[c])
        wide = dot(jnp.concatenate([high, low], 0), table_high[c])
        store[c] = wide[:rows] + (wide[rows:] + dot(high, table_low[c]))
        return carry

    lax.fori_loop(0, LEAD, step, 0, unroll=True)


def mix_left(store, table_high, table_low):
    cols = store.shape[2]

    def step(c, carry):
        high, low = halves(store[c])
        wide = dot(table_high[c], jnp.concatenate([high, low], 1))
        store[c] = wide[:, :cols] + (wide[:, cols:] + dot(table_low[c], high))
        return carry

    lax.fori_loop(0, LEAD, step, 0, unroll=True)


def lane_parts(col_shift):
    tile = lax.div(col_shift, LANES)
    return tile, col_shift - tile * LANES


def eight_rows(window, part, start, lanes):
    base = lax.div(start, 8) * 8
    shift = start - base
    after = jnp.minimum(base + 8, window.shape[1] - 8)
    back = lax.rem(8 - shift, 8)
    upper = pltpu.roll(window[part, pl.ds(pl.multiple_of(base, 8), 8), lanes], back, 0)
    lower = pltpu.roll(window[part, pl.ds(pl.multiple_of(after, 8), 8), lanes], back, 0)
    row = lax.broadcasted_iota(jnp.int32, upper.shape, 0)
    return jnp.where(row < 8 - shift, upper, lower)


def shifted_tiles(window, part, row_start, tile, shift):
    last = window.shape[2] // LANES - 1
    back = lax.rem(LANES - shift, LANES)
    lane = lax.broadcasted_iota(jnp.int32, (8, LANES), 1)
    rolled = []
    for j in range(LEAD + 1):
        at = pl.multiple_of(jnp.minimum(tile + j, last) * LANES, LANES)
        rolled.append(pltpu.roll(eight_rows(window, part, row_start, pl.ds(at, LANES)), back, 1))
    keep = lane < LANES - shift
    return [jnp.where(keep, rolled[j], rolled[j + 1]) for j in range(LEAD)]


def fetch(pairs, sems):
    copies = [pltpu.make_async_copy(src, dst, sems.at[n]) for n, (src, dst) in enumerate(pairs)]
    for copy in copies:
        copy.start()
    for copy in copies:
        copy.wait()


def exit_kernel(
    shifts, probe_r, probe_i, object_r, object_i, below_r, below_i, table_high, table_low, out,
    window, store, sems,
):
    fetch(
        [
            (object_r, window.at[0, pl.ds(0, ROWS)]),
            (object_i, window.at[1, pl.ds(0, ROWS)]),
            (below_r, window.at[0, pl.ds(ROWS, ROWS)]),
            (below_i, window.at[1, pl.ds(ROWS, ROWS)]),
        ],
        sems,
    )
    row_shift = shifts[0]
    tile, shift = lane_parts(shifts[1])

    def gather(k, carry):
        at = pl.multiple_of(k * 8, 8)
        rows = pl.ds(at, 8)
        patch_r = shifted_tiles(window, 0, row_shift + at, tile, shift)
        patch_i = shifted_tiles(window, 1, row_shift + at, tile, shift)
        values = []
        for a in range(LEAD):
            lanes = pl.ds(a * LANES, LANES)
            real, imag = probe_r[rows, lanes], probe_i[rows, lanes]
            values.append(
                (real * patch_r[a] - imag * patch_i[a], real * patch_i[a] + imag * patch_r[a])
            )
        for c, (real, imag) in enumerate(dft16(values, -1)):
            store[c, rows, pl.ds(0, LANES)] = real
            store[c, rows, pl.ds(LANES, LANES)] = imag
        return carry

    lax.fori_loop(0, ROWS // 8, gather, 0)
    mix_right(store, table_high, table_low)

    def spread(k, carry):
        rows = pl.ds(pl.multiple_of(k * 8, 8), 8)
        values = [(store[c, rows, pl.ds(0, LANES)], store[c, rows, pl.ds(LANES, LANES)]) for c in range(LEAD)]
        for a, (real, imag) in enumerate(dft16(values, 1)):
            out[a, 0, rows] = real
            out[a, 1, rows] = imag
        return carry

    lax.fori_loop(0, ROWS // 8, spread, 0)


def detector_kernel(shifts, columns, measured, table_high, table_low, out, store, wrapped):
    row_shift = shifts[0]

    def load(c, k):
        at = pl.multiple_of(k * 8, 8)
        return (store[c, pl.ds(at, 8)], store[c, pl.ds(pl.multiple_of(ROWS + k * 8, 8), 8)])

    def save(values, k):
        for c, (real, imag) in enumerate(values):
            store[c, pl.ds(pl.multiple_of(k * 8, 8), 8)] = real
            store[c, pl.ds(pl.multiple_of(ROWS + k * 8, 8), 8)] = imag

    def first(k, carry):
        rows = pl.ds(pl.multiple_of(k * 8, 8), 8)
        save(dft16([(columns[a, 0, rows], columns[a, 1, rows]) for a in range(LEAD)], -1), k)
        return carry

    lax.fori_loop(0, ROWS // 8, first, 0)
    mix_left(store, table_high, table_low)

    def modulus(k, carry):
        rows = pl.ds(pl.multiple_of(k * 8, 8), 8)
        residual = []
        for a, (real, imag) in enumerate(dft16([load(c, k) for c in range(LEAD)], 1)):
            share = measured[a, rows] * lax.rsqrt(jnp.maximum(real * real + imag * imag, 0.0625))
            keep = 1.0 - share
            residual.append((real * keep, -imag * keep))
        save(dft16(residual, -1), k)
        return carry

    lax.fori_loop(0, ROWS // 8, modulus, 0)
    mix_left(store, table_high, table_low)

    def last(k, carry):
        for a, (real, imag) in enumerate(dft16([load(c, k) for c in range(LEAD)], 1)):
            at = pl.multiple_of((a + 1) * ROWS + k * 8, 8)
            wrapped[0, pl.ds(at, 8)] = real
            wrapped[1, pl.ds(at, 8)] = -imag
            if a == LEAD - 1:
                first_at = pl.multiple_of(k * 8, 8)
                wrapped[0, pl.ds(first_at, 8)] = real
                wrapped[1, pl.ds(first_at, 8)] = -imag
        return carry

    lax.fori_loop(0, ROWS // 8, last, 0)

    def place(n, carry):
        part = lax.div(n, LEAD)
        start = ROWS * (n - part * LEAD + 1) + PART * part
        aligned = pl.multiple_of(start, 8)
        for half in range(2):
            out[n, half] = wrapped[half, pl.ds(aligned, PART)]
            for k in range(PART // 8):
                out[n, 2 + half, pl.ds(8 * k, 8)] = eight_rows(
                    wrapped, half, start - row_shift + 8 * k, slice(None)
                )
        return carry

    lax.fori_loop(0, GROUP * LEAD, place, 0)


def gradient_kernel(
    shifts, rows_in, probe_r, probe_i, above_r, above_i, object_r, object_i, below_r, below_i,
    table_high, table_low, out, probe_window, object_window, store, probe_acc, object_acc, sems,
):
    fetch(
        [
            (above_r, probe_window.at[0, pl.ds(0, ROWS)]),
            (above_i, probe_window.at[1, pl.ds(0, ROWS)]),
            (probe_r, probe_window.at[0, pl.ds(ROWS, ROWS)]),
            (probe_i, probe_window.at[1, pl.ds(ROWS, ROWS)]),
            (object_r, object_window.at[0, pl.ds(0, ROWS)]),
            (object_i, object_window.at[1, pl.ds(0, ROWS)]),
            (below_r, object_window.at[0, pl.ds(ROWS, ROWS)]),
            (below_i, object_window.at[1, pl.ds(ROWS, ROWS)]),
        ],
        sems,
    )
    own = shifts[2 * GROUP]
    own_start = own * PART
    chunks = PART // 8

    def first(m, carry):
        aligned = lax.div(m, GROUP * chunks)
        position = lax.rem(lax.div(m, chunks), GROUP)
        rows = pl.ds(pl.multiple_of(lax.rem(m, chunks) * 8, 8), 8)
        at = pl.ds(pl.multiple_of(m * 8, 8), 8)
        values = [
            (rows_in[position * LEAD + a, 2 * aligned, rows], -rows_in[position * LEAD + a, 2 * aligned + 1, rows])
            for a in range(LEAD)
        ]
        for c, (real, imag) in enumerate(dft16(values, -1)):
            store[c, at, pl.ds(0, LANES)] = real
            store[c, at, pl.ds(LANES, LANES)] = imag
        return carry

    lax.fori_loop(0, 2 * GROUP * chunks, first, 0)
    mix_right(store, table_high, table_low)
    probe_acc[...] = jnp.zeros_like(probe_acc)
    object_acc[...] = jnp.zeros_like(object_acc)

    def back(m):
        at = pl.ds(pl.multiple_of(m * 8, 8), 8)
        values = [(store[c, at, pl.ds(0, LANES)], store[c, at, pl.ds(LANES, LANES)]) for c in range(LEAD)]
        return [(real, -imag) for real, imag in dft16(values, 1)]

    def probe_term(m, carry):
        position = lax.div(m, chunks)
        offset = pl.multiple_of(lax.rem(m, chunks) * 8, 8)
        rows = pl.ds(offset, 8)
        entry = 2 * lax.bitwise_xor(own, position)
        tile, shift = lane_parts(shifts[entry + 1])
        start = own_start + shifts[entry] + offset
        patch_r = shifted_tiles(object_window, 0, start, tile, shift)
        patch_i = shifted_tiles(object_window, 1, start, tile, shift)
        for a, (real, imag) in enumerate(back(m)):
            lanes = pl.ds(a * LANES, LANES)
            probe_acc[0, rows, lanes] += patch_r[a] * real + patch_i[a] * imag
            probe_acc[1, rows, lanes] += patch_r[a] * imag - patch_i[a] * real
        return carry

    lax.fori_loop(0, GROUP * chunks, probe_term, 0)
    lane = lax.broadcasted_iota(jnp.int32, (8, LANES), 1)

    def object_term(m, carry):
        position = lax.div(m, chunks)
        offset = pl.multiple_of(lax.rem(m, chunks) * 8, 8)
        rows = pl.ds(offset, 8)
        entry = 2 * lax.bitwise_xor(own, position)
        tile, shift = lane_parts(shifts[entry + 1])
        start = ROWS + own_start - shifts[entry] + offset
        rolled = []
        for a, (real, imag) in enumerate(back(GROUP * chunks + m)):
            lanes = pl.ds(a * LANES, LANES)
            probe_real = eight_rows(probe_window, 0, start, lanes)
            probe_imag = eight_rows(probe_window, 1, start, lanes)
            rolled.append(
                (
                    pltpu.roll(probe_real * real + probe_imag * imag, shift, 1),
                    pltpu.roll(probe_real * imag - probe_imag * real, shift, 1),
                )
            )
        keep = lane >= shift
        for j in range(LEAD + 1):
            lanes = pl.ds(pl.multiple_of((tile + j) * LANES, LANES), LANES)
            for half in range(2):
                here = rolled[j][half] if j < LEAD else 0.0
                left = rolled[j - 1][half] if j > 0 else 0.0
                object_acc[half, rows, lanes] += jnp.where(keep, here, left)
        return carry

    lax.fori_loop(0, GROUP * chunks, object_term, 0)
    own = object_acc.shape[2] // LANES * LANES
    width = LANES + LANES // 8
    for b in range(LEAD):
        for half in range(2):
            out[b, pl.ds(half * PART, PART)] = probe_acc[half, :, pl.ds(b * LANES, LANES)]
            out[b, pl.ds((2 + half) * PART, PART)] = object_acc[half, :, pl.ds(b * width, LANES)]
        pieces = []
        for k in range(chunks):
            for half in range(2):
                pieces.append(object_acc[half, pl.ds(8 * k, 8), pl.ds(b * width + LANES, width - LANES)])
        out[b, pl.ds(4 * PART, 8)] = jnp.concatenate(pieces, 1)


def total_kernel(terms, probe_r, probe_i, object_r, object_i):
    width = LANES // 8
    totals = []
    for part in range(GROUP):
        total = terms[part]
        for high in range(1, LEAD // GROUP):
            total = total + terms[high * GROUP + part]
        totals.append(total)
    for half, (probe_out, object_out) in enumerate(((probe_r, object_r), (probe_i, object_i))):
        for part in range(GROUP):
            probe_out[pl.ds(part * PART, PART)] = totals[part][half * PART : (half + 1) * PART]
        left = [totals[part][(2 + half) * PART : (3 + half) * PART] for part in range(GROUP)]
        object_out[pl.ds(0, LANES)] = jnp.concatenate(left, 0).T
        right = []
        for part in range(GROUP):
            for k in range(PART // 8):
                at = (2 * k + half) * width
                right.append(totals[part][4 * PART : 4 * PART + 8, at : at + width])
        object_out[pl.ds(LANES, width)] = jnp.concatenate(right, 0).T


SMEM = pl.BlockSpec(memory_space=pltpu.SMEM)
VMEM = pl.BlockSpec(memory_space=pltpu.VMEM)
ANY = pl.BlockSpec(memory_space=pl.ANY)
PARAMS = pltpu.CompilerParams(vmem_limit_bytes=VMEM_LIMIT)


def shape(*sizes):
    return jax.ShapeDtypeStruct(sizes, F32)


def passed_along(value, by):
    size = lax.axis_size("row")
    return lax.ppermute(value, "row", [(i, (i + by) % size) for i in range(size)])


def per_device(tables, probe_r, probe_i, object_r, object_i, amplitudes, row_shift, col_shift):
    right_high, right_low, left_high, left_low = tables
    width = object_r.shape[1]
    field = probe_r.shape[1]
    group = ("zl", "yl")
    below_r, below_i = passed_along(object_r, -1), passed_along(object_i, -1)
    own = lax.axis_index(group).astype(jnp.int32)
    own_shift = jnp.concatenate([row_shift, col_shift])
    others = [
        lax.ppermute(own_shift, group, [(i, i ^ by) for i in range(GROUP)]) for by in range(1, GROUP)
    ]
    all_shifts = jnp.concatenate([own_shift] + others + [own[None]])
    measured = amplitudes[0].reshape(ROWS, LEAD, LANES).transpose(1, 0, 2)
    measured = lax.all_to_all(measured, "row", 0, 0, tiled=True)

    below_r, below_i, late_r, late_i = lax.optimization_barrier((below_r, below_i, probe_r, probe_i))
    above_r, above_i = passed_along(late_r, 1), passed_along(late_i, 1)
    exit_spread = pl.pallas_call(
        exit_kernel,
        out_shape=shape(LEAD, 2, ROWS, LANES),
        in_specs=[SMEM, VMEM, VMEM, ANY, ANY, ANY, ANY, VMEM, VMEM],
        out_specs=VMEM,
        scratch_shapes=[
            pltpu.VMEM((2, 2 * ROWS, width), F32),
            pltpu.VMEM((LEAD, ROWS, 2 * LANES), F32),
            pltpu.SemaphoreType.DMA((4,)),
        ],
        compiler_params=PARAMS,
        name="exit_kernel",
    )(all_shifts, probe_r, probe_i, object_r, object_i, below_r, below_i, right_high, right_low)
    columns = lax.all_to_all(exit_spread, "row", 0, 0, tiled=True)
    columns, above_r, above_i = lax.optimization_barrier((columns, above_r, above_i))
    returned = pl.pallas_call(
        detector_kernel,
        out_shape=shape(GROUP * LEAD, 4, PART, LANES),
        in_specs=[SMEM, VMEM, VMEM, VMEM, VMEM],
        out_specs=VMEM,
        scratch_shapes=[
            pltpu.VMEM((LEAD, 2 * ROWS, LANES), F32),
            pltpu.VMEM((2, (LEAD + 1) * ROWS, LANES), F32),
        ],
        compiler_params=PARAMS,
        name="detector_kernel",
    )(all_shifts, columns, measured, left_high, left_low)
    rows_in = lax.all_to_all(returned, group + ("row",), 0, 0, tiled=True)
    terms = pl.pallas_call(
        gradient_kernel,
        out_shape=shape(LEAD, 4 * PART + 8, LANES),
        in_specs=[SMEM, VMEM] + [ANY] * 8 + [VMEM, VMEM],
        out_specs=VMEM,
        scratch_shapes=[
            pltpu.VMEM((2, 2 * ROWS, field), F32),
            pltpu.VMEM((2, 2 * ROWS, width), F32),
            pltpu.VMEM((LEAD, 2 * ROWS, 2 * LANES), F32),
            pltpu.VMEM((2, PART, field), F32),
            pltpu.VMEM((2, PART, width + LANES), F32),
            pltpu.SemaphoreType.DMA((8,)),
        ],
        compiler_params=PARAMS,
        name="gradient_kernel",
    )(
        all_shifts, rows_in, probe_r, probe_i, above_r, above_i, object_r, object_i, below_r, below_i,
        right_high, right_low,
    )
    terms = lax.all_to_all(terms, ("zh",) + group, 0, 0, tiled=True)
    own_width = width // LEAD
    probe_r, probe_i, object_r, object_i = pl.pallas_call(
        total_kernel,
        out_shape=(shape(ROWS, LANES), shape(ROWS, LANES), shape(own_width, ROWS), shape(own_width, ROWS)),
        in_specs=[VMEM],
        out_specs=(VMEM, VMEM, VMEM, VMEM),
        compiler_params=PARAMS,
        name="total_kernel",
    )(terms)
    return probe_r, probe_i, object_r.T, object_i.T


def solution(mesh):
    fine = Mesh(mesh.devices.reshape(4, 2, 2, LEAD), ("zh", "zl", "yl", "row"))
    batch = ("zh", "zl", "yl")
    tables = propagation_tables(LEAD * LANES)

    def step(*arguments):
        held = tuple(jnp.asarray(table) for table in tables)
        return functools.partial(per_device, held)(*arguments)

    placed = (
        P("row", None),
        P("row", None),
        P("row", None),
        P("row", None),
        P(batch, "row", None),
        P(batch),
        P(batch),
    )
    return jax.shard_map(
        step,
        mesh=fine,
        in_specs=placed,
        out_specs=(P("row", batch),) * 4,
        check_vma=False,
    )
```

```python
import functools
import math

import jax
import jax.numpy as jnp
import ml_dtypes
import numpy as np
from jax import lax
from jax.experimental import pallas as pl
from jax.experimental.pallas import tpu as pltpu
from jax.sharding import Mesh, PartitionSpec as P

F32 = jnp.float32
BF16 = jnp.bfloat16
LANES = 128
LEAD = 16
ROWS = 128
GROUP = 4
PART = ROWS // GROUP
MEBI = 1024 * 1024


def split_pair(table):
    high = table.astype(ml_dtypes.bfloat16)
    low = (table - high.astype(np.float64)).astype(ml_dtypes.bfloat16)
    return high, low


@functools.lru_cache(maxsize=None)
def propagation_tables(length):
    index = np.arange(length, dtype=np.int64)
    frequency = np.where(index < length // 2, index, index - length)
    chirp = np.exp(-2j * np.pi * ((frequency * frequency) % (4 * length)) / (4 * length))
    offsets = np.arange(-(LANES - 1), LANES, dtype=np.int64)
    place = np.arange(LANES)
    right = np.empty((LEAD, 2 * LANES, 2 * LANES))
    for c in range(LEAD):
        tone = c + LEAD * np.arange(LANES, dtype=np.int64)
        phase = np.exp(2j * np.pi * ((offsets[:, None] * tone[None, :]) % length) / length)
        line = phase @ chirp[tone] / length
        middle = line[place[:, None] - place[None, :] + LANES - 1]
        left = np.block([[middle.real, -middle.imag], [middle.imag, middle.real]])
        right[c] = left.T
    return split_pair(right) + split_pair(np.ascontiguousarray(np.swapaxes(right, 1, 2)))


def times(value, cosine, sine):
    real, imag = value
    if sine == 0.0 and cosine == 1.0:
        return value
    if cosine == 0.0 and sine == -1.0:
        return (imag, -real)
    if cosine == 0.0 and sine == 1.0:
        return (-imag, real)
    return (real * cosine - imag * sine, real * sine + imag * cosine)


def add(left, right):
    return (left[0] + right[0], left[1] + right[1])


def sub(left, right):
    return (left[0] - right[0], left[1] - right[1])


def dft4(values, sign):
    a, b, c, d = values
    even, odd = add(a, c), sub(a, c)
    both, gap = add(b, d), sub(b, d)
    turned = (-sign * gap[1], sign * gap[0]) if sign < 0 else (-gap[1], gap[0])
    if sign < 0:
        turned = (gap[1], -gap[0])
    return [add(even, both), add(odd, turned), sub(even, both), sub(odd, turned)]


def dft16(values, sign):
    inner = [dft4([values[4 * n1 + n2] for n1 in range(4)], sign) for n2 in range(4)]
    result = [None] * 16
    for k1 in range(4):
        column = []
        for n2 in range(4):
            turns = n2 * k1 % 16
            angle = 2.0 * math.pi * turns / 16
            cosine, sine = math.cos(angle), sign * math.sin(angle)
            if turns in (0, 4, 8, 12):
                cosine, sine = float(round(cosine)), float(round(sine))
            column.append(times(inner[n2][k1], cosine, sine))
        for k2, value in enumerate(dft4(column, sign)):
            result[k1 + 4 * k2] = value
    return result


def halves(value):
    high = value.astype(BF16)
    return high, (value - high.astype(F32)).astype(BF16)


def dot(left, right):
    return jnp.dot(left, right, preferred_element_type=F32)


def mix_right(store, table_high, table_low):
    rows = store.shape[1]

    def step(c, carry):
        high, low = halves(store[c])
        wide = dot(jnp.concatenate([high, low], 0), table_high[c])
        store[c] = wide[:rows] + (wide[rows:] + dot(high, table_low[c]))
        return carry

    lax.fori_loop(0, LEAD, step, 0, unroll=True)


def mix_left(store, table_high, table_low):
    cols = store.shape[2]

    def step(c, carry):
        high, low = halves(store[c])
        wide = dot(table_high[c], jnp.concatenate([high, low], 1))
        store[c] = wide[:, :cols] + (wide[:, cols:] + dot(table_low[c], high))
        return carry

    lax.fori_loop(0, LEAD, step, 0, unroll=True)


def lane_parts(col_shift):
    tile = lax.div(col_shift, LANES)
    return tile, col_shift - tile * LANES


def eight_rows(window, part, start, lanes):
    base = lax.div(start, 8) * 8
    shift = start - base
    after = jnp.minimum(base + 8, window.shape[1] - 8)
    back = lax.rem(8 - shift, 8)
    upper = pltpu.roll(window[part, pl.ds(pl.multiple_of(base, 8), 8), lanes], back, 0)
    lower = pltpu.roll(window[part, pl.ds(pl.multiple_of(after, 8), 8), lanes], back, 0)
    row = lax.broadcasted_iota(jnp.int32, upper.shape, 0)
    return jnp.where(row < 8 - shift, upper, lower)


def shifted_tiles(window, part, row_start, tile, shift):
    last = window.shape[2] // LANES - 1
    back = lax.rem(LANES - shift, LANES)
    lane = lax.broadcasted_iota(jnp.int32, (8, LANES), 1)
    rolled = []
    for j in range(LEAD + 1):
        at = pl.multiple_of(jnp.minimum(tile + j, last) * LANES, LANES)
        rolled.append(pltpu.roll(eight_rows(window, part, row_start, pl.ds(at, LANES)), back, 1))
    keep = lane < LANES - shift
    return [jnp.where(keep, rolled[j], rolled[j + 1]) for j in range(LEAD)]


def block_copies(window, block, at, sems):
    rows = block[0].shape[0]
    return [
        pltpu.make_async_copy(block[half], window.at[half, pl.ds(at, rows)], sems.at[half])
        for half in range(2)
    ]


def halo_copies(window, halo, at, shifts, sems):
    near = block_copies(window, halo[:2], at, sems.at[0])
    far = []
    for by in range(GROUP):
        part = halo[2 + by]
        place = pl.multiple_of(at + PART * lax.bitwise_xor(shifts[2 * GROUP + 2], by), PART)
        far += block_copies(window, (part.at[0], part.at[1]), place, sems.at[by])
    return near, far


def run_all(copies, method):
    for copy in copies:
        getattr(copy, method)()


def run_halo(copies, from_chip, method):
    @pl.when(from_chip)
    def _():
        run_all(copies[0], method)

    @pl.when(jnp.logical_not(from_chip))
    def _():
        run_all(copies[1], method)


def exit_kernel(
    shifts, probe_r, probe_i, object_r, object_i, below_r, below_i, measured, high_in, low_in, out,
    window, probe, table_high, table_low, store, spread, sems, table_sems, measured_sems, out_sems,
):
    fields = block_copies(window, (object_r, object_i), 0, sems.at[0])
    fields += block_copies(window, (below_r, below_i), ROWS, sems.at[1])
    fields += block_copies(probe, (probe_r, probe_i), 0, sems.at[2])
    tables = [
        pltpu.make_async_copy(source, target, table_sems.at[n])
        for n, (source, target) in enumerate(((high_in, table_high), (low_in, table_low)))
    ]
    passing = [
        pltpu.make_async_copy(measured.at[0, :, pl.ds(a * LANES, LANES)], spread.at[a, 2], measured_sems.at[a])
        for a in range(LEAD)
    ]
    run_all(fields, "start")
    run_all(tables, "start")
    run_all(passing, "start")
    run_all(fields, "wait")
    row_shift = shifts[0]
    tile, shift = lane_parts(shifts[1])

    def gather(k, carry):
        at = pl.multiple_of(k * 8, 8)
        rows = pl.ds(at, 8)
        patch_r = shifted_tiles(window, 0, row_shift + at, tile, shift)
        patch_i = shifted_tiles(window, 1, row_shift + at, tile, shift)
        values = []
        for a in range(LEAD):
            lanes = pl.ds(a * LANES, LANES)
            real, imag = probe[0, rows, lanes], probe[1, rows, lanes]
            values.append(
                (real * patch_r[a] - imag * patch_i[a], real * patch_i[a] + imag * patch_r[a])
            )
        for c, (real, imag) in enumerate(dft16(values, -1)):
            store[c, rows, pl.ds(0, LANES)] = real
            store[c, rows, pl.ds(LANES, LANES)] = imag
        return carry

    lax.fori_loop(0, ROWS // 8, gather, 0)
    run_all(tables, "wait")
    mix_right(store, table_high, table_low)

    def scatter(k, carry):
        rows = pl.ds(pl.multiple_of(k * 8, 8), 8)
        values = [(store[c, rows, pl.ds(0, LANES)], store[c, rows, pl.ds(LANES, LANES)]) for c in range(LEAD)]
        for a, (real, imag) in enumerate(dft16(values, 1)):
            spread[a, 0, rows] = real
            spread[a, 1, rows] = imag
        return carry

    run_all(passing, "wait")
    sends = []
    for part in range(GROUP):
        lax.fori_loop(part * PART // 8, (part + 1) * PART // 8, scatter, 0)
        rows = pl.ds(part * PART, PART)
        send = pltpu.make_async_copy(spread.at[:, :, rows], out.at[:, :, rows], out_sems.at[part])
        send.start()
        sends.append(send)
    run_all(sends, "wait")


def detector_kernel(
    shifts, columns_in, high_in, low_in, out, columns, table_high, table_low, store, wrapped, straight,
    shifted, sems, table_sems, out_sems,
):
    pieces = [pl.ds(part * PART, PART) for part in range(GROUP)]
    arriving = [
        pltpu.make_async_copy(columns_in.at[:, :, rows], columns.at[:, :, rows], sems.at[part])
        for part, rows in enumerate(pieces)
    ]
    tables = [
        pltpu.make_async_copy(source, target, table_sems.at[n])
        for n, (source, target) in enumerate(((high_in, table_high), (low_in, table_low)))
    ]
    run_all(arriving, "start")
    run_all(tables, "start")

    def load(c, k):
        at = pl.multiple_of(k * 8, 8)
        return (store[c, pl.ds(at, 8)], store[c, pl.ds(pl.multiple_of(ROWS + k * 8, 8), 8)])

    def save(values, k):
        for c, (real, imag) in enumerate(values):
            store[c, pl.ds(pl.multiple_of(k * 8, 8), 8)] = real
            store[c, pl.ds(pl.multiple_of(ROWS + k * 8, 8), 8)] = imag

    def first(k, carry):
        rows = pl.ds(pl.multiple_of(k * 8, 8), 8)
        save(dft16([(columns[a, 0, rows], columns[a, 1, rows]) for a in range(LEAD)], -1), k)
        return carry

    for part in range(GROUP):
        arriving[part].wait()
        lax.fori_loop(part * PART // 8, (part + 1) * PART // 8, first, 0)
    run_all(tables, "wait")
    mix_left(store, table_high, table_low)

    def modulus(k, carry):
        rows = pl.ds(pl.multiple_of(k * 8, 8), 8)
        residual = []
        for a, (real, imag) in enumerate(dft16([load(c, k) for c in range(LEAD)], 1)):
            share = columns[a, 2, rows] * lax.rsqrt(jnp.maximum(real * real + imag * imag, 0.0625))
            keep = 1.0 - share
            residual.append((real * keep, -imag * keep))
        save(dft16(residual, -1), k)
        return carry

    lax.fori_loop(0, ROWS // 8, modulus, 0)
    mix_left(store, table_high, table_low)

    def last(k, carry):
        rows = pl.ds(pl.multiple_of(k * 8, 8), 8)
        for a, (real, imag) in enumerate(dft16([load(c, k) for c in range(LEAD)], 1)):
            at = pl.multiple_of((a + 1) * ROWS + k * 8, 8)
            for half, value in enumerate((real, -imag)):
                straight[half, a, rows] = value
                wrapped[half, pl.ds(at, 8)] = value
                if a == LEAD - 1:
                    wrapped[half, rows] = value
        return carry

    sends = []

    def send(source, half, part):
        target = out.at[pl.ds(part * LEAD, LEAD), half]
        copy = pltpu.make_async_copy(source.at[half % 2, :, pieces[part]], target, out_sems.at[half, part])
        copy.start()
        sends.append(copy)

    for part in range(GROUP):
        lax.fori_loop(part * PART // 8, (part + 1) * PART // 8, last, 0)
        send(straight, 0, part)
        send(straight, 1, part)
    base = lax.div(shifts[0] + 7, 8) * 8
    keep = lax.broadcasted_iota(jnp.int32, (8, LANES), 0) < 8 - (base - shifts[0])
    back = lax.rem(8 - (base - shifts[0]), 8)
    limit = wrapped.shape[1] - 8

    for part in range(GROUP):

        def place(a, carry):
            start = (a + 1) * ROWS + part * PART - base
            for half in range(2):
                rolled = []
                for k in range(PART // 8 + 1):
                    at = pl.multiple_of(jnp.minimum(start + 8 * k, limit), 8)
                    rolled.append(pltpu.roll(wrapped[half, pl.ds(at, 8)], back, 0))
                for k in range(PART // 8):
                    rows = pl.ds(part * PART + 8 * k, 8)
                    shifted[half, a, rows] = jnp.where(keep, rolled[k], rolled[k + 1])
            return carry

        lax.fori_loop(0, LEAD, place, 0)
        send(shifted, 2, part)
        send(shifted, 3, part)
    run_all(sends, "wait")


def gradient_kernel(shifts, rows_in, *refs):
    halo = 2 + GROUP
    object_own, object_below = refs[2 + halo : 4 + halo], refs[4 + halo : 6 + halo]
    table_high, table_low, out = refs[6 + halo : 9 + halo]
    probe_window, object_window, store, probe_acc, object_acc, sems, halo_sems = refs[9 + halo :]
    core = shifts[2 * GROUP + 1]
    held = block_copies(probe_window, refs[:2], ROWS, sems.at[0])
    held += block_copies(object_window, object_own, 0, sems.at[1])
    held += block_copies(object_window, object_below, ROWS, sems.at[2])
    moved = halo_copies(probe_window, refs[2 : 2 + halo], 0, shifts, halo_sems)
    run_all(held, "start")
    run_halo(moved, core == 1, "start")
    own = shifts[2 * GROUP]
    own_start = own * PART
    chunks = PART // 8

    def first(m, carry):
        aligned = lax.div(m, GROUP * chunks)
        position = lax.rem(lax.div(m, chunks), GROUP)
        rows = pl.ds(pl.multiple_of(lax.rem(m, chunks) * 8, 8), 8)
        at = pl.ds(pl.multiple_of(m * 8, 8), 8)
        values = [
            (rows_in[position * LEAD + a, 2 * aligned, rows], -rows_in[position * LEAD + a, 2 * aligned + 1, rows])
            for a in range(LEAD)
        ]
        for c, (real, imag) in enumerate(dft16(values, -1)):
            store[c, at, pl.ds(0, LANES)] = real
            store[c, at, pl.ds(LANES, LANES)] = imag
        return carry

    lax.fori_loop(0, 2 * GROUP * chunks, first, 0)
    mix_right(store, table_high, table_low)
    run_all(held, "wait")
    run_halo(moved, core == 1, "wait")
    probe_acc[...] = jnp.zeros_like(probe_acc)
    object_acc[...] = jnp.zeros_like(object_acc)

    def back(m):
        at = pl.ds(pl.multiple_of(m * 8, 8), 8)
        values = [(store[c, at, pl.ds(0, LANES)], store[c, at, pl.ds(LANES, LANES)]) for c in range(LEAD)]
        return [(real, -imag) for real, imag in dft16(values, 1)]

    def probe_term(m, carry):
        position = lax.div(m, chunks)
        offset = pl.multiple_of(lax.rem(m, chunks) * 8, 8)
        rows = pl.ds(offset, 8)
        entry = 2 * lax.bitwise_xor(own, position)
        tile, shift = lane_parts(shifts[entry + 1])
        start = own_start + shifts[entry] + offset
        patch_r = shifted_tiles(object_window, 0, start, tile, shift)
        patch_i = shifted_tiles(object_window, 1, start, tile, shift)
        for a, (real, imag) in enumerate(back(m)):
            lanes = pl.ds(a * LANES, LANES)
            probe_acc[0, rows, lanes] += patch_r[a] * real + patch_i[a] * imag
            probe_acc[1, rows, lanes] += patch_r[a] * imag - patch_i[a] * real
        return carry

    lax.fori_loop(0, GROUP * chunks, probe_term, 0)
    lane = lax.broadcasted_iota(jnp.int32, (8, LANES), 1)

    def object_term(m, carry):
        position = lax.div(m, chunks)
        offset = pl.multiple_of(lax.rem(m, chunks) * 8, 8)
        rows = pl.ds(offset, 8)
        entry = 2 * lax.bitwise_xor(own, position)
        tile, shift = lane_parts(shifts[entry + 1])
        start = ROWS + own_start - shifts[entry] + offset
        rolled = []
        for a, (real, imag) in enumerate(back(GROUP * chunks + m)):
            lanes = pl.ds(a * LANES, LANES)
            probe_real = eight_rows(probe_window, 0, start, lanes)
            probe_imag = eight_rows(probe_window, 1, start, lanes)
            rolled.append(
                (
                    pltpu.roll(probe_real * real + probe_imag * imag, shift, 1),
                    pltpu.roll(probe_real * imag - probe_imag * real, shift, 1),
                )
            )
        keep = lane >= shift
        for j in range(LEAD + 1):
            lanes = pl.ds(pl.multiple_of((tile + j) * LANES, LANES), LANES)
            for half in range(2):
                here = rolled[j][half] if j < LEAD else 0.0
                left = rolled[j - 1][half] if j > 0 else 0.0
                object_acc[half, rows, lanes] += jnp.where(keep, here, left)
        return carry

    lax.fori_loop(0, GROUP * chunks, object_term, 0)
    own = object_acc.shape[2] // LANES * LANES
    width = LANES + LANES // 8
    for b in range(LEAD):
        for half in range(2):
            out[b, pl.ds(half * PART, PART)] = probe_acc[half, :, pl.ds(b * LANES, LANES)]
            out[b, pl.ds((2 + half) * PART, PART)] = object_acc[half, :, pl.ds(b * width, LANES)]
        pieces = []
        for k in range(chunks):
            for half in range(2):
                pieces.append(object_acc[half, pl.ds(8 * k, 8), pl.ds(b * width + LANES, width - LANES)])
        out[b, pl.ds(4 * PART, 8)] = jnp.concatenate(pieces, 1)


def total_kernel(terms, probe_r, probe_i, object_r, object_i):
    width = LANES // 8
    totals = []
    for part in range(GROUP):
        total = terms[part]
        for high in range(1, LEAD // GROUP):
            total = total + terms[high * GROUP + part]
        totals.append(total)
    for half, (probe_out, object_out) in enumerate(((probe_r, object_r), (probe_i, object_i))):
        for part in range(GROUP):
            probe_out[pl.ds(part * PART, PART)] = totals[part][half * PART : (half + 1) * PART]
        left = [totals[part][(2 + half) * PART : (3 + half) * PART] for part in range(GROUP)]
        object_out[pl.ds(0, LANES)] = jnp.concatenate(left, 0).T
        right = []
        for part in range(GROUP):
            for k in range(PART // 8):
                at = (2 * k + half) * width
                right.append(totals[part][4 * PART : 4 * PART + 8, at : at + width])
        object_out[pl.ds(LANES, width)] = jnp.concatenate(right, 0).T


SMEM = pl.BlockSpec(memory_space=pltpu.SMEM)
VMEM = pl.BlockSpec(memory_space=pltpu.VMEM)
ANY = pl.BlockSpec(memory_space=pl.ANY)


def params(mebibytes):
    return pltpu.CompilerParams(vmem_limit_bytes=mebibytes * MEBI)


def shape(*sizes):
    return jax.ShapeDtypeStruct(sizes, F32)


def row_pairs(by, inside):
    pairs = [(r, (r + by) % LEAD) for r in range(LEAD)]
    return [(a, b) for a, b in pairs if (a // 2 == b // 2) == inside]


def fetched_part():
    return lax.axis_index(("zh", "zl")) % GROUP


def own_part(real, imag):
    at = fetched_part() * PART
    return jnp.stack([lax.dynamic_slice_in_dim(value, at, PART, 0) for value in (real, imag)])


def passed_on(part, takers):
    parts = [part]
    for by in range(1, GROUP):
        pairs = [(z * LEAD + r, (z ^ by) * LEAD + r) for z in range(8) for r in takers]
        parts.append(lax.ppermute(part, ("zh", "zl", "row"), pairs))
    return tuple(parts)


def together(*values):
    return lax.optimization_barrier(values)


def per_device(tables, probe_r, probe_i, object_r, object_i, amplitudes, row_shift, col_shift):
    right_high, right_low, left_high, left_low = tables
    width = object_r.shape[1]
    field = probe_r.shape[1]
    group = ("zl", "yl")
    below_r, below_i = (
        lax.ppermute(value, "row", row_pairs(-1, False) + row_pairs(-1, True)) for value in (object_r, object_i)
    )
    own = lax.axis_index(group).astype(jnp.int32)
    core = lax.axis_index("row").astype(jnp.int32) % 2
    part = fetched_part().astype(jnp.int32)
    own_shift = jnp.concatenate([row_shift, col_shift])
    others = [
        lax.ppermute(own_shift, group, [(i, i ^ by) for i in range(GROUP)]) for by in range(1, GROUP)
    ]
    all_shifts = jnp.concatenate([own_shift] + others + [own[None], core[None], part[None]])
    above_part = own_part(probe_r, probe_i)
    near_above = tuple(lax.ppermute(value, "row", row_pairs(1, True)) for value in (probe_r, probe_i))
    below_r, below_i, above_part, all_shifts, near_above = together(
        below_r, below_i, above_part, all_shifts, near_above
    )
    above_part = lax.ppermute(above_part, "row", row_pairs(1, False))
    exit_spread = pl.pallas_call(
        exit_kernel,
        out_shape=shape(LEAD, 3, ROWS, LANES),
        in_specs=[SMEM, ANY, ANY, ANY, ANY, ANY, ANY, ANY, ANY, ANY],
        out_specs=ANY,
        scratch_shapes=[
            pltpu.VMEM((2, 2 * ROWS, width), F32),
            pltpu.VMEM((2, ROWS, field), F32),
            pltpu.VMEM(right_high.shape, BF16),
            pltpu.VMEM(right_low.shape, BF16),
            pltpu.VMEM((LEAD, ROWS, 2 * LANES), F32),
            pltpu.VMEM((LEAD, 3, ROWS, LANES), F32),
            pltpu.SemaphoreType.DMA((3, 2)),
            pltpu.SemaphoreType.DMA((2,)),
            pltpu.SemaphoreType.DMA((LEAD,)),
            pltpu.SemaphoreType.DMA((GROUP,)),
        ],
        compiler_params=params(60),
        cost_estimate=pl.CostEstimate(flops=int(2e9), bytes_accessed=int(20e6), transcendentals=0),
        name="exit_kernel",
    )(
        all_shifts, probe_r, probe_i, object_r, object_i, below_r, below_i, amplitudes, right_high,
        right_low,
    )
    exit_spread, above_part = together(exit_spread, above_part)
    columns = lax.all_to_all(exit_spread, "row", 0, 0, tiled=True)
    above = passed_on(above_part, range(0, LEAD, 2))
    returned = pl.pallas_call(
        detector_kernel,
        out_shape=shape(GROUP * LEAD, 4, PART, LANES),
        in_specs=[SMEM, ANY, ANY, ANY],
        out_specs=ANY,
        scratch_shapes=[
            pltpu.VMEM((LEAD, 3, ROWS, LANES), F32),
            pltpu.VMEM(left_high.shape, BF16),
            pltpu.VMEM(left_low.shape, BF16),
            pltpu.VMEM((LEAD, 2 * ROWS, LANES), F32),
            pltpu.VMEM((2, (LEAD + 1) * ROWS, LANES), F32),
            pltpu.VMEM((2, LEAD, ROWS, LANES), F32),
            pltpu.VMEM((2, LEAD, ROWS, LANES), F32),
            pltpu.SemaphoreType.DMA((GROUP,)),
            pltpu.SemaphoreType.DMA((2,)),
            pltpu.SemaphoreType.DMA((4, GROUP)),
        ],
        compiler_params=params(60),
        cost_estimate=pl.CostEstimate(flops=4000000000, bytes_accessed=36000000, transcendentals=0),
        name="detector_kernel",
    )(all_shifts, columns, left_high, left_low)
    returned, above = together(returned, above)
    rows_in = lax.all_to_all(returned, group + ("row",), 0, 0, tiled=True)
    terms = pl.pallas_call(
        gradient_kernel,
        out_shape=shape(LEAD, 4 * PART + 8, LANES),
        in_specs=[SMEM, VMEM] + [ANY] * (8 + GROUP) + [VMEM, VMEM],
        out_specs=VMEM,
        scratch_shapes=[
            pltpu.VMEM((2, 2 * ROWS, field), F32),
            pltpu.VMEM((2, 2 * ROWS, width), F32),
            pltpu.VMEM((LEAD, 2 * ROWS, 2 * LANES), F32),
            pltpu.VMEM((2, PART, field), F32),
            pltpu.VMEM((2, PART, width + LANES), F32),
            pltpu.SemaphoreType.DMA((3, 2)),
            pltpu.SemaphoreType.DMA((GROUP, 2)),
        ],
        compiler_params=params(28),
        cost_estimate=pl.CostEstimate(flops=4000000000, bytes_accessed=50000000, transcendentals=0),
        name="gradient_kernel",
    )(
        all_shifts, rows_in, probe_r, probe_i, *near_above, *above, object_r, object_i, below_r, below_i,
        right_high, right_low,
    )
    terms = lax.all_to_all(terms, ("zh",) + group, 0, 0, tiled=True)
    own_width = width // LEAD
    probe_r, probe_i, object_r, object_i = pl.pallas_call(
        total_kernel,
        out_shape=(shape(ROWS, LANES), shape(ROWS, LANES), shape(own_width, ROWS), shape(own_width, ROWS)),
        in_specs=[VMEM],
        out_specs=(VMEM, VMEM, VMEM, VMEM),
        compiler_params=params(8),
        cost_estimate=pl.CostEstimate(flops=10000000, bytes_accessed=6000000, transcendentals=0),
        name="total_kernel",
    )(terms)
    return probe_r, probe_i, object_r.T, object_i.T


def solution(mesh):
    fine = Mesh(mesh.devices.reshape(4, 2, 2, LEAD), ("zh", "zl", "yl", "row"))
    batch = ("zh", "zl", "yl")
    tables = propagation_tables(LEAD * LANES)

    def step(*arguments):
        held = tuple(jnp.asarray(table) for table in tables)
        return functools.partial(per_device, held)(*arguments)

    placed = (
        P("row", None),
        P("row", None),
        P("row", None),
        P("row", None),
        P(batch, "row", None),
        P(batch),
        P(batch),
    )
    return jax.shard_map(
        step,
        mesh=fine,
        in_specs=placed,
        out_specs=(P("row", batch),) * 4,
        check_vma=False,
    )
```

```python
import functools
import math

import jax
import jax.numpy as jnp
import ml_dtypes
import numpy as np
from jax import lax
from jax.experimental import pallas as pl
from jax.experimental.pallas import tpu as pltpu
from jax.sharding import Mesh, PartitionSpec as P

F32 = jnp.float32
BF16 = jnp.bfloat16
LANES = 128
LEAD = 16
ROWS = 128
GROUP = 4
UNROLL = 4
PART = ROWS // GROUP
MEBI = 1024 * 1024


def split_pair(table):
    high = table.astype(ml_dtypes.bfloat16)
    low = (table - high.astype(np.float64)).astype(ml_dtypes.bfloat16)
    return high, low


@functools.lru_cache(maxsize=None)
def propagation_tables(length):
    index = np.arange(length, dtype=np.int64)
    frequency = np.where(index < length // 2, index, index - length)
    chirp = np.exp(-2j * np.pi * ((frequency * frequency) % (4 * length)) / (4 * length))
    offsets = np.arange(-(LANES - 1), LANES, dtype=np.int64)
    place = np.arange(LANES)
    right = np.empty((LEAD, 2 * LANES, 2 * LANES))
    for c in range(LEAD):
        tone = c + LEAD * np.arange(LANES, dtype=np.int64)
        phase = np.exp(2j * np.pi * ((offsets[:, None] * tone[None, :]) % length) / length)
        line = phase @ chirp[tone] / length
        middle = line[place[:, None] - place[None, :] + LANES - 1]
        left = np.block([[middle.real, -middle.imag], [middle.imag, middle.real]])
        right[c] = left.T
    return split_pair(right) + split_pair(np.ascontiguousarray(np.swapaxes(right, 1, 2)))


def times(value, cosine, sine):
    real, imag = value
    if sine == 0.0 and cosine == 1.0:
        return value
    if cosine == 0.0 and sine == -1.0:
        return (imag, -real)
    if cosine == 0.0 and sine == 1.0:
        return (-imag, real)
    return (real * cosine - imag * sine, real * sine + imag * cosine)


def add(left, right):
    return (left[0] + right[0], left[1] + right[1])


def sub(left, right):
    return (left[0] - right[0], left[1] - right[1])


def dft4(values, sign):
    a, b, c, d = values
    even, odd = add(a, c), sub(a, c)
    both, gap = add(b, d), sub(b, d)
    turned = (-sign * gap[1], sign * gap[0]) if sign < 0 else (-gap[1], gap[0])
    if sign < 0:
        turned = (gap[1], -gap[0])
    return [add(even, both), add(odd, turned), sub(even, both), sub(odd, turned)]


def dft16(values, sign):
    inner = [dft4([values[4 * n1 + n2] for n1 in range(4)], sign) for n2 in range(4)]
    result = [None] * 16
    for k1 in range(4):
        column = []
        for n2 in range(4):
            turns = n2 * k1 % 16
            angle = 2.0 * math.pi * turns / 16
            cosine, sine = math.cos(angle), sign * math.sin(angle)
            if turns in (0, 4, 8, 12):
                cosine, sine = float(round(cosine)), float(round(sine))
            column.append(times(inner[n2][k1], cosine, sine))
        for k2, value in enumerate(dft4(column, sign)):
            result[k1 + 4 * k2] = value
    return result


def halves(value):
    high = value.astype(BF16)
    return high, (value - high.astype(F32)).astype(BF16)


def dot(left, right):
    return jnp.dot(left, right, preferred_element_type=F32)


def mix_right(store, table_high, table_low):
    rows = store.shape[1]

    def step(c, carry):
        high, low = halves(store[c])
        wide = dot(jnp.concatenate([high, low], 0), table_high[c])
        store[c] = wide[:rows] + (wide[rows:] + dot(high, table_low[c]))
        return carry

    lax.fori_loop(0, LEAD, step, 0, unroll=True)


def mix_left(store, table_high, table_low):
    cols = store.shape[2]

    def step(c, carry):
        high, low = halves(store[c])
        wide = dot(table_high[c], jnp.concatenate([high, low], 1))
        store[c] = wide[:, :cols] + (wide[:, cols:] + dot(table_low[c], high))
        return carry

    lax.fori_loop(0, LEAD, step, 0, unroll=True)


def lane_parts(col_shift):
    tile = lax.div(col_shift, LANES)
    return tile, col_shift - tile * LANES


def eight_rows(window, part, start, lanes):
    base = lax.div(start, 8) * 8
    shift = start - base
    after = jnp.minimum(base + 8, window.shape[1] - 8)
    back = lax.rem(8 - shift, 8)
    upper = pltpu.roll(window[part, pl.ds(pl.multiple_of(base, 8), 8), lanes], back, 0)
    lower = pltpu.roll(window[part, pl.ds(pl.multiple_of(after, 8), 8), lanes], back, 0)
    row = lax.broadcasted_iota(jnp.int32, upper.shape, 0)
    return jnp.where(row < 8 - shift, upper, lower)


def shifted_tiles(window, part, row_start, tile, shift):
    last = window.shape[2] // LANES - 1
    back = lax.rem(LANES - shift, LANES)
    lane = lax.broadcasted_iota(jnp.int32, (8, LANES), 1)
    rolled = []
    for j in range(LEAD + 1):
        at = pl.multiple_of(jnp.minimum(tile + j, last) * LANES, LANES)
        rolled.append(pltpu.roll(eight_rows(window, part, row_start, pl.ds(at, LANES)), back, 1))
    keep = lane < LANES - shift
    return [jnp.where(keep, rolled[j], rolled[j + 1]) for j in range(LEAD)]


def block_copies(window, block, at, sems):
    rows = block[0].shape[0]
    return [
        pltpu.make_async_copy(block[half], window.at[half, pl.ds(at, rows)], sems.at[half])
        for half in range(2)
    ]


def halo_copies(window, halo, at, shifts, sems):
    near = block_copies(window, halo[:2], at, sems.at[0])
    far = []
    for by in range(GROUP):
        part = halo[2 + by]
        place = pl.multiple_of(at + PART * lax.bitwise_xor(shifts[2 * GROUP + 2], by), PART)
        far += block_copies(window, (part.at[0], part.at[1]), place, sems.at[by])
    return near, far


def run_all(copies, method):
    for copy in copies:
        getattr(copy, method)()


def run_halo(copies, from_chip, method):
    @pl.when(from_chip)
    def _():
        run_all(copies[0], method)

    @pl.when(jnp.logical_not(from_chip))
    def _():
        run_all(copies[1], method)


def part_kernel(place, real, imag, out, sems):
    rows = pl.ds(pl.multiple_of(place[0] * PART, PART), PART)
    copies = block_copies(out, (real.at[rows], imag.at[rows]), 0, sems)
    run_all(copies, "start")
    run_all(copies, "wait")


def exit_kernel(
    shifts, probe_r, probe_i, object_r, object_i, below_r, below_i, measured, high_in, low_in, out,
    window, probe, table_high, table_low, store, spread, sems, table_sems, measured_sems, out_sems,
):
    held = block_copies(window, (object_r, object_i), 0, sems.at[0])
    pieces = []
    for part in range(GROUP):
        rows = pl.ds(part * PART, PART)
        piece = block_copies(
            window, (below_r.at[rows], below_i.at[rows]), ROWS + part * PART, sems.at[1 + part]
        )
        pieces.append(
            piece + block_copies(probe, (probe_r.at[rows], probe_i.at[rows]), part * PART, sems.at[5 + part])
        )
    tables = [
        pltpu.make_async_copy(source, target, table_sems.at[n])
        for n, (source, target) in enumerate(((high_in, table_high), (low_in, table_low)))
    ]
    passing = [
        pltpu.make_async_copy(measured.at[0, :, pl.ds(a * LANES, LANES)], spread.at[a, 2], measured_sems.at[a])
        for a in range(LEAD)
    ]
    run_all(held, "start")
    for piece in pieces:
        run_all(piece, "start")
    run_all(tables, "start")
    run_all(passing, "start")
    run_all(held, "wait")
    row_shift = shifts[0]
    tile, shift = lane_parts(shifts[1])

    def gather(k, carry):
        at = pl.multiple_of(k * 8, 8)
        rows = pl.ds(at, 8)
        patch_r = shifted_tiles(window, 0, row_shift + at, tile, shift)
        patch_i = shifted_tiles(window, 1, row_shift + at, tile, shift)
        values = []
        for a in range(LEAD):
            lanes = pl.ds(a * LANES, LANES)
            real, imag = probe[0, rows, lanes], probe[1, rows, lanes]
            values.append(
                (real * patch_r[a] - imag * patch_i[a], real * patch_i[a] + imag * patch_r[a])
            )
        for c, (real, imag) in enumerate(dft16(values, -1)):
            store[c, rows, pl.ds(0, LANES)] = real
            store[c, rows, pl.ds(LANES, LANES)] = imag
        return carry

    for part in range(GROUP):
        run_all(pieces[part], "wait")
        lax.fori_loop(part * PART // 8, (part + 1) * PART // 8, gather, 0, unroll=UNROLL)
    run_all(tables, "wait")
    mix_right(store, table_high, table_low)

    def scatter(k, carry):
        rows = pl.ds(pl.multiple_of(k * 8, 8), 8)
        values = [(store[c, rows, pl.ds(0, LANES)], store[c, rows, pl.ds(LANES, LANES)]) for c in range(LEAD)]
        for a, (real, imag) in enumerate(dft16(values, 1)):
            spread[a, 0, rows] = real
            spread[a, 1, rows] = imag
        return carry

    run_all(passing, "wait")
    sends = []
    for part in range(GROUP):
        lax.fori_loop(part * PART // 8, (part + 1) * PART // 8, scatter, 0, unroll=UNROLL)
        rows = pl.ds(part * PART, PART)
        send = pltpu.make_async_copy(spread.at[:, :, rows], out.at[:, :, rows], out_sems.at[part])
        send.start()
        sends.append(send)
    run_all(sends, "wait")


def detector_kernel(
    shifts, columns_in, high_in, low_in, out, columns, table_high, table_low, store, wrapped, straight,
    shifted, sems, table_sems, out_sems,
):
    pieces = [pl.ds(part * PART, PART) for part in range(GROUP)]
    arriving = [
        pltpu.make_async_copy(columns_in.at[:, :, rows], columns.at[:, :, rows], sems.at[part])
        for part, rows in enumerate(pieces)
    ]
    tables = [
        pltpu.make_async_copy(source, target, table_sems.at[n])
        for n, (source, target) in enumerate(((high_in, table_high), (low_in, table_low)))
    ]
    run_all(arriving, "start")
    run_all(tables, "start")

    def load(c, k):
        at = pl.multiple_of(k * 8, 8)
        return (store[c, pl.ds(at, 8)], store[c, pl.ds(pl.multiple_of(ROWS + k * 8, 8), 8)])

    def save(values, k):
        for c, (real, imag) in enumerate(values):
            store[c, pl.ds(pl.multiple_of(k * 8, 8), 8)] = real
            store[c, pl.ds(pl.multiple_of(ROWS + k * 8, 8), 8)] = imag

    def first(k, carry):
        rows = pl.ds(pl.multiple_of(k * 8, 8), 8)
        save(dft16([(columns[a, 0, rows], columns[a, 1, rows]) for a in range(LEAD)], -1), k)
        return carry

    for part in range(GROUP):
        arriving[part].wait()
        lax.fori_loop(part * PART // 8, (part + 1) * PART // 8, first, 0, unroll=UNROLL)
    run_all(tables, "wait")
    mix_left(store, table_high, table_low)

    def modulus(k, carry):
        rows = pl.ds(pl.multiple_of(k * 8, 8), 8)
        residual = []
        for a, (real, imag) in enumerate(dft16([load(c, k) for c in range(LEAD)], 1)):
            share = columns[a, 2, rows] * lax.rsqrt(jnp.maximum(real * real + imag * imag, 0.0625))
            keep = 1.0 - share
            residual.append((real * keep, -imag * keep))
        save(dft16(residual, -1), k)
        return carry

    lax.fori_loop(0, ROWS // 8, modulus, 0, unroll=UNROLL)
    mix_left(store, table_high, table_low)

    def last(k, carry):
        rows = pl.ds(pl.multiple_of(k * 8, 8), 8)
        for a, (real, imag) in enumerate(dft16([load(c, k) for c in range(LEAD)], 1)):
            at = pl.multiple_of((a + 1) * ROWS + k * 8, 8)
            for half, value in enumerate((real, -imag)):
                straight[half, a, rows] = value
                wrapped[half, pl.ds(at, 8)] = value
                if a == LEAD - 1:
                    wrapped[half, rows] = value
        return carry

    sends = []

    def send(source, half, part):
        target = out.at[pl.ds(part * LEAD, LEAD), half]
        copy = pltpu.make_async_copy(source.at[half % 2, :, pieces[part]], target, out_sems.at[half, part])
        copy.start()
        sends.append(copy)

    for part in range(GROUP):
        lax.fori_loop(part * PART // 8, (part + 1) * PART // 8, last, 0, unroll=UNROLL)
        send(straight, 0, part)
        send(straight, 1, part)
    base = lax.div(shifts[0] + 7, 8) * 8
    keep = lax.broadcasted_iota(jnp.int32, (8, LANES), 0) < 8 - (base - shifts[0])
    back = lax.rem(8 - (base - shifts[0]), 8)
    limit = wrapped.shape[1] - 8

    for part in range(GROUP):

        def place(a, carry):
            start = (a + 1) * ROWS + part * PART - base
            for half in range(2):
                rolled = []
                for k in range(PART // 8 + 1):
                    at = pl.multiple_of(jnp.minimum(start + 8 * k, limit), 8)
                    rolled.append(pltpu.roll(wrapped[half, pl.ds(at, 8)], back, 0))
                for k in range(PART // 8):
                    rows = pl.ds(part * PART + 8 * k, 8)
                    shifted[half, a, rows] = jnp.where(keep, rolled[k], rolled[k + 1])
            return carry

        lax.fori_loop(0, LEAD, place, 0, unroll=UNROLL)
        send(shifted, 2, part)
        send(shifted, 3, part)
    run_all(sends, "wait")


def gradient_kernel(shifts, rows_in, *refs):
    halo = 2 + GROUP
    object_own, object_below = refs[2 + halo : 4 + halo], refs[4 + halo : 6 + halo]
    table_high, table_low, out = refs[6 + halo : 9 + halo]
    probe_window, object_window, store, probe_acc, object_acc, sems, halo_sems = refs[9 + halo :]
    core = shifts[2 * GROUP + 1]
    held = block_copies(probe_window, refs[:2], ROWS, sems.at[0])
    held += block_copies(object_window, object_own, 0, sems.at[1])
    held += block_copies(object_window, object_below, ROWS, sems.at[2])
    moved = halo_copies(probe_window, refs[2 : 2 + halo], 0, shifts, halo_sems)
    run_all(held, "start")
    run_halo(moved, core == 1, "start")
    own = shifts[2 * GROUP]
    own_start = own * PART
    chunks = PART // 8

    def first(m, carry):
        aligned = lax.div(m, GROUP * chunks)
        position = lax.rem(lax.div(m, chunks), GROUP)
        rows = pl.ds(pl.multiple_of(lax.rem(m, chunks) * 8, 8), 8)
        at = pl.ds(pl.multiple_of(m * 8, 8), 8)
        values = [
            (rows_in[position * LEAD + a, 2 * aligned, rows], -rows_in[position * LEAD + a, 2 * aligned + 1, rows])
            for a in range(LEAD)
        ]
        for c, (real, imag) in enumerate(dft16(values, -1)):
            store[c, at, pl.ds(0, LANES)] = real
            store[c, at, pl.ds(LANES, LANES)] = imag
        return carry

    lax.fori_loop(0, 2 * GROUP * chunks, first, 0, unroll=UNROLL)
    mix_right(store, table_high, table_low)
    run_all(held, "wait")
    run_halo(moved, core == 1, "wait")
    probe_acc[...] = jnp.zeros_like(probe_acc)
    object_acc[...] = jnp.zeros_like(object_acc)

    def back(m):
        at = pl.ds(pl.multiple_of(m * 8, 8), 8)
        values = [(store[c, at, pl.ds(0, LANES)], store[c, at, pl.ds(LANES, LANES)]) for c in range(LEAD)]
        return [(real, -imag) for real, imag in dft16(values, 1)]

    def probe_term(m, carry):
        position = lax.div(m, chunks)
        offset = pl.multiple_of(lax.rem(m, chunks) * 8, 8)
        rows = pl.ds(offset, 8)
        entry = 2 * lax.bitwise_xor(own, position)
        tile, shift = lane_parts(shifts[entry + 1])
        start = own_start + shifts[entry] + offset
        patch_r = shifted_tiles(object_window, 0, start, tile, shift)
        patch_i = shifted_tiles(object_window, 1, start, tile, shift)
        for a, (real, imag) in enumerate(back(m)):
            lanes = pl.ds(a * LANES, LANES)
            probe_acc[0, rows, lanes] += patch_r[a] * real + patch_i[a] * imag
            probe_acc[1, rows, lanes] += patch_r[a] * imag - patch_i[a] * real
        return carry

    lax.fori_loop(0, GROUP * chunks, probe_term, 0, unroll=UNROLL)
    lane = lax.broadcasted_iota(jnp.int32, (8, LANES), 1)

    def object_term(m, carry):
        position = lax.div(m, chunks)
        offset = pl.multiple_of(lax.rem(m, chunks) * 8, 8)
        rows = pl.ds(offset, 8)
        entry = 2 * lax.bitwise_xor(own, position)
        tile, shift = lane_parts(shifts[entry + 1])
        start = ROWS + own_start - shifts[entry] + offset
        rolled = []
        for a, (real, imag) in enumerate(back(GROUP * chunks + m)):
            lanes = pl.ds(a * LANES, LANES)
            probe_real = eight_rows(probe_window, 0, start, lanes)
            probe_imag = eight_rows(probe_window, 1, start, lanes)
            rolled.append(
                (
                    pltpu.roll(probe_real * real + probe_imag * imag, shift, 1),
                    pltpu.roll(probe_real * imag - probe_imag * real, shift, 1),
                )
            )
        keep = lane >= shift
        for j in range(LEAD + 1):
            lanes = pl.ds(pl.multiple_of((tile + j) * LANES, LANES), LANES)
            for half in range(2):
                here = rolled[j][half] if j < LEAD else 0.0
                left = rolled[j - 1][half] if j > 0 else 0.0
                object_acc[half, rows, lanes] += jnp.where(keep, here, left)
        return carry

    lax.fori_loop(0, GROUP * chunks, object_term, 0, unroll=UNROLL)
    own = object_acc.shape[2] // LANES * LANES
    width = LANES + LANES // 8
    for b in range(LEAD):
        for half in range(2):
            out[b, pl.ds(half * PART, PART)] = probe_acc[half, :, pl.ds(b * LANES, LANES)]
            out[b, pl.ds((2 + half) * PART, PART)] = object_acc[half, :, pl.ds(b * width, LANES)]
        pieces = []
        for k in range(chunks):
            for half in range(2):
                pieces.append(object_acc[half, pl.ds(8 * k, 8), pl.ds(b * width + LANES, width - LANES)])
        out[b, pl.ds(4 * PART, 8)] = jnp.concatenate(pieces, 1)


def total_kernel(terms, probe_r, probe_i, object_r, object_i):
    width = LANES // 8
    totals = []
    for part in range(GROUP):
        total = terms[part]
        for high in range(1, LEAD // GROUP):
            total = total + terms[high * GROUP + part]
        totals.append(total)
    for half, (probe_out, object_out) in enumerate(((probe_r, object_r), (probe_i, object_i))):
        for part in range(GROUP):
            probe_out[pl.ds(part * PART, PART)] = totals[part][half * PART : (half + 1) * PART]
        left = [totals[part][(2 + half) * PART : (3 + half) * PART] for part in range(GROUP)]
        object_out[pl.ds(0, LANES)] = jnp.concatenate(left, 0).T
        right = []
        for part in range(GROUP):
            for k in range(PART // 8):
                at = (2 * k + half) * width
                right.append(totals[part][4 * PART : 4 * PART + 8, at : at + width])
        object_out[pl.ds(LANES, width)] = jnp.concatenate(right, 0).T


SMEM = pl.BlockSpec(memory_space=pltpu.SMEM)
VMEM = pl.BlockSpec(memory_space=pltpu.VMEM)
ANY = pl.BlockSpec(memory_space=pl.ANY)


def params(mebibytes):
    return pltpu.CompilerParams(vmem_limit_bytes=mebibytes * MEBI)


def shape(*sizes):
    return jax.ShapeDtypeStruct(sizes, F32)


def row_pairs(by, inside):
    pairs = [(r, (r + by) % LEAD) for r in range(LEAD)]
    return [(a, b) for a, b in pairs if (a // 2 == b // 2) == inside]


def fetched_part():
    return lax.axis_index(("zh", "zl")) % GROUP


def own_part(place, real, imag):
    return pl.pallas_call(
        part_kernel,
        out_shape=shape(2, PART, real.shape[1]),
        in_specs=[SMEM, ANY, ANY],
        out_specs=VMEM,
        scratch_shapes=[pltpu.SemaphoreType.DMA((2,))],
        compiler_params=params(4),
        name="part_kernel",
    )(place, real, imag)


def passed_on(part, takers):
    parts = [part]
    for by in range(1, GROUP):
        pairs = []
        for z in range(8):
            for yl in range(2):
                if z % GROUP >= 2 * ((z ^ by) % 2) + yl:
                    pairs += [((2 * z + yl) * LEAD + r, (2 * (z ^ by) + yl) * LEAD + r) for r in takers]
        parts.append(lax.ppermute(part, ("zh", "zl", "yl", "row"), pairs))
    return tuple(parts)


def together(*values):
    return lax.optimization_barrier(values)


def per_device(tables, probe_r, probe_i, object_r, object_i, amplitudes, row_shift, col_shift):
    right_high, right_low, left_high, left_low = tables
    width = object_r.shape[1]
    field = probe_r.shape[1]
    group = ("zl", "yl")
    below_r, below_i = (
        lax.ppermute(value, "row", row_pairs(-1, False) + row_pairs(-1, True)) for value in (object_r, object_i)
    )
    own = lax.axis_index(group).astype(jnp.int32)
    core = lax.axis_index("row").astype(jnp.int32) % 2
    part = fetched_part().astype(jnp.int32)
    own_shift = jnp.concatenate([row_shift, col_shift])
    others = [
        lax.ppermute(own_shift, group, [(i, i ^ by) for i in range(GROUP)]) for by in range(1, GROUP)
    ]
    all_shifts = jnp.concatenate([own_shift] + others + [own[None], core[None], part[None]])
    above_part = own_part(part[None], probe_r, probe_i)
    near_above = tuple(lax.ppermute(value, "row", row_pairs(1, True)) for value in (probe_r, probe_i))
    below_r, below_i, above_part, all_shifts, near_above = together(
        below_r, below_i, above_part, all_shifts, near_above
    )
    above_part = lax.ppermute(above_part, "row", row_pairs(1, False))
    exit_spread = pl.pallas_call(
        exit_kernel,
        out_shape=shape(LEAD, 3, ROWS, LANES),
        in_specs=[SMEM, ANY, ANY, ANY, ANY, ANY, ANY, ANY, ANY, ANY],
        out_specs=ANY,
        scratch_shapes=[
            pltpu.VMEM((2, 2 * ROWS, width), F32),
            pltpu.VMEM((2, ROWS, field), F32),
            pltpu.VMEM(right_high.shape, BF16),
            pltpu.VMEM(right_low.shape, BF16),
            pltpu.VMEM((LEAD, ROWS, 2 * LANES), F32),
            pltpu.VMEM((LEAD, 3, ROWS, LANES), F32),
            pltpu.SemaphoreType.DMA((1 + 2 * GROUP, 2)),
            pltpu.SemaphoreType.DMA((2,)),
            pltpu.SemaphoreType.DMA((LEAD,)),
            pltpu.SemaphoreType.DMA((GROUP,)),
        ],
        compiler_params=params(60),
        cost_estimate=pl.CostEstimate(flops=int(2e9), bytes_accessed=int(20e6), transcendentals=0),
        name="exit_kernel",
    )(
        all_shifts, probe_r, probe_i, object_r, object_i, below_r, below_i, amplitudes, right_high,
        right_low,
    )
    exit_spread, above_part = together(exit_spread, above_part)
    columns = lax.all_to_all(exit_spread, "row", 0, 0, tiled=True)
    above = passed_on(above_part, range(0, LEAD, 2))
    returned = pl.pallas_call(
        detector_kernel,
        out_shape=shape(GROUP * LEAD, 4, PART, LANES),
        in_specs=[SMEM, ANY, ANY, ANY],
        out_specs=ANY,
        scratch_shapes=[
            pltpu.VMEM((LEAD, 3, ROWS, LANES), F32),
            pltpu.VMEM(left_high.shape, BF16),
            pltpu.VMEM(left_low.shape, BF16),
            pltpu.VMEM((LEAD, 2 * ROWS, LANES), F32),
            pltpu.VMEM((2, (LEAD + 1) * ROWS, LANES), F32),
            pltpu.VMEM((2, LEAD, ROWS, LANES), F32),
            pltpu.VMEM((2, LEAD, ROWS, LANES), F32),
            pltpu.SemaphoreType.DMA((GROUP,)),
            pltpu.SemaphoreType.DMA((2,)),
            pltpu.SemaphoreType.DMA((4, GROUP)),
        ],
        compiler_params=params(60),
        cost_estimate=pl.CostEstimate(flops=4000000000, bytes_accessed=36000000, transcendentals=0),
        name="detector_kernel",
    )(all_shifts, columns, left_high, left_low)
    returned, above = together(returned, above)
    rows_in = lax.all_to_all(returned, group + ("row",), 0, 0, tiled=True)
    terms = pl.pallas_call(
        gradient_kernel,
        out_shape=shape(LEAD, 4 * PART + 8, LANES),
        in_specs=[SMEM, VMEM] + [ANY] * (8 + GROUP) + [VMEM, VMEM],
        out_specs=VMEM,
        scratch_shapes=[
            pltpu.VMEM((2, 2 * ROWS, field), F32),
            pltpu.VMEM((2, 2 * ROWS, width), F32),
            pltpu.VMEM((LEAD, 2 * ROWS, 2 * LANES), F32),
            pltpu.VMEM((2, PART, field), F32),
            pltpu.VMEM((2, PART, width + LANES), F32),
            pltpu.SemaphoreType.DMA((3, 2)),
            pltpu.SemaphoreType.DMA((GROUP, 2)),
        ],
        compiler_params=params(28),
        cost_estimate=pl.CostEstimate(flops=4000000000, bytes_accessed=50000000, transcendentals=0),
        name="gradient_kernel",
    )(
        all_shifts, rows_in, probe_r, probe_i, *near_above, *above, object_r, object_i, below_r, below_i,
        right_high, right_low,
    )
    terms = lax.all_to_all(terms, ("zh",) + group, 0, 0, tiled=True)
    own_width = width // LEAD
    probe_r, probe_i, object_r, object_i = pl.pallas_call(
        total_kernel,
        out_shape=(shape(ROWS, LANES), shape(ROWS, LANES), shape(own_width, ROWS), shape(own_width, ROWS)),
        in_specs=[VMEM],
        out_specs=(VMEM, VMEM, VMEM, VMEM),
        compiler_params=params(8),
        cost_estimate=pl.CostEstimate(flops=10000000, bytes_accessed=6000000, transcendentals=0),
        name="total_kernel",
    )(terms)
    return probe_r, probe_i, object_r.T, object_i.T


def solution(mesh):
    fine = Mesh(mesh.devices.reshape(4, 2, 2, LEAD), ("zh", "zl", "yl", "row"))
    batch = ("zh", "zl", "yl")
    tables = propagation_tables(LEAD * LANES)

    def step(*arguments):
        held = tuple(jnp.asarray(table) for table in tables)
        return functools.partial(per_device, held)(*arguments)

    placed = (
        P("row", None),
        P("row", None),
        P("row", None),
        P("row", None),
        P(batch, "row", None),
        P(batch),
        P(batch),
    )
    return jax.shard_map(
        step,
        mesh=fine,
        in_specs=placed,
        out_specs=(P("row", batch),) * 4,
        check_vma=False,
    )
```

```python
import functools
import math

import jax
import jax.numpy as jnp
import ml_dtypes
import numpy as np
from jax import lax
from jax.experimental import pallas as pl
from jax.experimental.pallas import tpu as pltpu
from jax.sharding import Mesh, PartitionSpec as P

F32 = jnp.float32
BF16 = jnp.bfloat16
LANES = 128
LEAD = 16
ROWS = 128
GROUP = 4
UNROLL = 4
PART = ROWS // GROUP
MEBI = 1024 * 1024


def split_pair(table):
    high = table.astype(ml_dtypes.bfloat16)
    low = (table - high.astype(np.float64)).astype(ml_dtypes.bfloat16)
    return high, low


@functools.lru_cache(maxsize=None)
def propagation_tables(length):
    index = np.arange(length, dtype=np.int64)
    frequency = np.where(index < length // 2, index, index - length)
    chirp = np.exp(-2j * np.pi * ((frequency * frequency) % (4 * length)) / (4 * length))
    offsets = np.arange(-(LANES - 1), LANES, dtype=np.int64)
    place = np.arange(LANES)
    right, left = np.empty((LEAD, LANES, 2 * LANES)), np.empty((LEAD, LANES, 2 * LANES))
    for c in range(LEAD):
        tone = c + LEAD * np.arange(LANES, dtype=np.int64)
        phase = np.exp(2j * np.pi * ((offsets[:, None] * tone[None, :]) % length) / length)
        line = phase @ chirp[tone] / length
        middle = line[place[:, None] - place[None, :] + LANES - 1]
        right[c] = np.concatenate([middle.real.T, middle.imag.T], 1)
        left[c] = np.concatenate([middle.real, middle.imag], 1)
    return split_pair(right) + split_pair(left)


def times(value, cosine, sine):
    real, imag = value
    if sine == 0.0 and cosine == 1.0:
        return value
    if cosine == 0.0 and sine == -1.0:
        return (imag, -real)
    if cosine == 0.0 and sine == 1.0:
        return (-imag, real)
    return (real * cosine - imag * sine, real * sine + imag * cosine)


def add(left, right):
    return (left[0] + right[0], left[1] + right[1])


def sub(left, right):
    return (left[0] - right[0], left[1] - right[1])


def dft4(values, sign):
    a, b, c, d = values
    even, odd = add(a, c), sub(a, c)
    both, gap = add(b, d), sub(b, d)
    turned = (-sign * gap[1], sign * gap[0]) if sign < 0 else (-gap[1], gap[0])
    if sign < 0:
        turned = (gap[1], -gap[0])
    return [add(even, both), add(odd, turned), sub(even, both), sub(odd, turned)]


def dft16(values, sign):
    inner = [dft4([values[4 * n1 + n2] for n1 in range(4)], sign) for n2 in range(4)]
    result = [None] * 16
    for k1 in range(4):
        column = []
        for n2 in range(4):
            turns = n2 * k1 % 16
            angle = 2.0 * math.pi * turns / 16
            cosine, sine = math.cos(angle), sign * math.sin(angle)
            if turns in (0, 4, 8, 12):
                cosine, sine = float(round(cosine)), float(round(sine))
            column.append(times(inner[n2][k1], cosine, sine))
        for k2, value in enumerate(dft4(column, sign)):
            result[k1 + 4 * k2] = value
    return result


def halves(value):
    high = value.astype(BF16)
    return high, (value - high.astype(F32)).astype(BF16)


def dot(left, right):
    return jnp.dot(left, right, preferred_element_type=F32)


def right_block(pair):
    real, imag = pair[:, :LANES], pair[:, LANES:]
    return jnp.concatenate([pair, jnp.concatenate([-imag, real], 1)], 0)


def left_block(pair):
    real, imag = pair[:, :LANES], pair[:, LANES:]
    return jnp.concatenate([jnp.concatenate([real, -imag], 1), jnp.concatenate([imag, real], 1)], 0)


def mix_right(store, table_high, table_low):
    rows = store.shape[1]

    def step(c, carry):
        high, low = halves(store[c])
        wide = dot(jnp.concatenate([high, low], 0), right_block(table_high[c]))
        store[c] = wide[:rows] + (wide[rows:] + dot(high, right_block(table_low[c])))
        return carry

    lax.fori_loop(0, LEAD, step, 0, unroll=True)


def mix_left(store, table_high, table_low):
    cols = store.shape[2]

    def step(c, carry):
        high, low = halves(store[c])
        wide = dot(left_block(table_high[c]), jnp.concatenate([high, low], 1))
        store[c] = wide[:, :cols] + (wide[:, cols:] + dot(left_block(table_low[c]), high))
        return carry

    lax.fori_loop(0, LEAD, step, 0, unroll=True)


def lane_parts(col_shift):
    tile = lax.div(col_shift, LANES)
    return tile, col_shift - tile * LANES


def eight_rows(window, part, start, lanes):
    base = lax.div(start, 8) * 8
    shift = start - base
    after = jnp.minimum(base + 8, window.shape[1] - 8)
    back = lax.rem(8 - shift, 8)
    upper = pltpu.roll(window[part, pl.ds(pl.multiple_of(base, 8), 8), lanes], back, 0)
    lower = pltpu.roll(window[part, pl.ds(pl.multiple_of(after, 8), 8), lanes], back, 0)
    row = lax.broadcasted_iota(jnp.int32, upper.shape, 0)
    return jnp.where(row < 8 - shift, upper, lower)


def shifted_tiles(window, part, row_start, tile, shift):
    last = window.shape[2] // LANES - 1
    back = lax.rem(LANES - shift, LANES)
    lane = lax.broadcasted_iota(jnp.int32, (8, LANES), 1)
    rolled = []
    for j in range(LEAD + 1):
        at = pl.multiple_of(jnp.minimum(tile + j, last) * LANES, LANES)
        rolled.append(pltpu.roll(eight_rows(window, part, row_start, pl.ds(at, LANES)), back, 1))
    keep = lane < LANES - shift
    return [jnp.where(keep, rolled[j], rolled[j + 1]) for j in range(LEAD)]


def block_copies(window, block, at, sems):
    rows = block[0].shape[0]
    return [
        pltpu.make_async_copy(block[half], window.at[half, pl.ds(at, rows)], sems.at[half])
        for half in range(2)
    ]


def halo_copies(window, halo, at, shifts, sems):
    near = block_copies(window, halo[:2], at, sems.at[0])
    far = []
    for by in range(GROUP):
        part = halo[2 + by]
        place = pl.multiple_of(at + PART * lax.bitwise_xor(shifts[2 * GROUP + 2], by), PART)
        far += block_copies(window, (part.at[0], part.at[1]), place, sems.at[by])
    return near, far


def run_all(copies, method):
    for copy in copies:
        getattr(copy, method)()


def run_halo(copies, from_chip, method):
    @pl.when(from_chip)
    def _():
        run_all(copies[0], method)

    @pl.when(jnp.logical_not(from_chip))
    def _():
        run_all(copies[1], method)


def part_kernel(place, real, imag, out, sems):
    rows = pl.ds(pl.multiple_of(place[0] * PART, PART), PART)
    copies = block_copies(out, (real.at[rows], imag.at[rows]), 0, sems)
    run_all(copies, "start")
    run_all(copies, "wait")


def exit_kernel(
    shifts, probe_r, probe_i, object_r, object_i, below_r, below_i, measured, high_in, low_in, out,
    window, probe, table_high, table_low, store, spread, sems, table_sems, measured_sems, out_sems,
):
    row_shift = shifts[0]
    held, moved, pieces = [], [], []
    for part in range(GROUP):
        rows = pl.ds(part * PART, PART)
        held.append(block_copies(window, (object_r.at[rows], object_i.at[rows]), part * PART, sems.at[part]))
        moved.append(
            block_copies(window, (below_r.at[rows], below_i.at[rows]), ROWS + part * PART, sems.at[GROUP + part])
        )
        pieces.append(
            block_copies(probe, (probe_r.at[rows], probe_i.at[rows]), part * PART, sems.at[2 * GROUP + part])
        )

    def run_held(part, method):
        @pl.when(row_shift < (part + 1) * PART)
        def _():
            run_all(held[part], method)

    def run_moved(part, method):
        @pl.when(row_shift > part * PART)
        def _():
            run_all(moved[part], method)

    tables = [
        pltpu.make_async_copy(source, target, table_sems.at[n])
        for n, (source, target) in enumerate(((high_in, table_high), (low_in, table_low)))
    ]
    passing = [
        pltpu.make_async_copy(measured.at[0, :, pl.ds(a * LANES, LANES)], spread.at[a, 2], measured_sems.at[a])
        for a in range(LEAD)
    ]
    for part in range(GROUP):
        run_held(part, "start")
    for part in range(GROUP):
        run_moved(part, "start")
        run_all(pieces[part], "start")
    run_all(tables, "start")
    run_all(passing, "start")
    for part in range(GROUP):
        run_held(part, "wait")
    tile, shift = lane_parts(shifts[1])

    def gather(k, carry):
        at = pl.multiple_of(k * 8, 8)
        rows = pl.ds(at, 8)
        patch_r = shifted_tiles(window, 0, row_shift + at, tile, shift)
        patch_i = shifted_tiles(window, 1, row_shift + at, tile, shift)
        values = []
        for a in range(LEAD):
            lanes = pl.ds(a * LANES, LANES)
            real, imag = probe[0, rows, lanes], probe[1, rows, lanes]
            values.append(
                (real * patch_r[a] - imag * patch_i[a], real * patch_i[a] + imag * patch_r[a])
            )
        for c, (real, imag) in enumerate(dft16(values, -1)):
            store[c, rows, pl.ds(0, LANES)] = real
            store[c, rows, pl.ds(LANES, LANES)] = imag
        return carry

    for part in range(GROUP):
        run_moved(part, "wait")
        run_all(pieces[part], "wait")
        lax.fori_loop(part * PART // 8, (part + 1) * PART // 8, gather, 0, unroll=UNROLL)
    run_all(tables, "wait")
    mix_right(store, table_high, table_low)

    def scatter(k, carry):
        rows = pl.ds(pl.multiple_of(k * 8, 8), 8)
        values = [(store[c, rows, pl.ds(0, LANES)], store[c, rows, pl.ds(LANES, LANES)]) for c in range(LEAD)]
        for a, (real, imag) in enumerate(dft16(values, 1)):
            spread[a, 0, rows] = real
            spread[a, 1, rows] = imag
        return carry

    run_all(passing, "wait")
    sends = []
    for part in range(GROUP):
        lax.fori_loop(part * PART // 8, (part + 1) * PART // 8, scatter, 0, unroll=UNROLL)
        rows = pl.ds(part * PART, PART)
        send = pltpu.make_async_copy(spread.at[:, :, rows], out.at[:, :, rows], out_sems.at[part])
        send.start()
        sends.append(send)
    run_all(sends, "wait")


def detector_kernel(
    shifts, columns_in, high_in, low_in, out, columns, table_high, table_low, store, wrapped, straight,
    shifted, sems, table_sems, out_sems,
):
    pieces = [pl.ds(part * PART, PART) for part in range(GROUP)]
    arriving = [
        pltpu.make_async_copy(
            columns_in.at[:, pl.ds(0, 2), rows], columns.at[:, pl.ds(0, 2), rows], sems.at[part]
        )
        for part, rows in enumerate(pieces)
    ]
    tables = [
        pltpu.make_async_copy(source, target, table_sems.at[n])
        for n, (source, target) in enumerate(((high_in, table_high), (low_in, table_low)))
    ]
    measured = pltpu.make_async_copy(columns_in.at[:, 2], columns.at[:, 2], table_sems.at[2])
    run_all(arriving, "start")
    run_all(tables, "start")
    measured.start()

    def load(c, k):
        at = pl.multiple_of(k * 8, 8)
        return (store[c, pl.ds(at, 8)], store[c, pl.ds(pl.multiple_of(ROWS + k * 8, 8), 8)])

    def save(values, k):
        for c, (real, imag) in enumerate(values):
            store[c, pl.ds(pl.multiple_of(k * 8, 8), 8)] = real
            store[c, pl.ds(pl.multiple_of(ROWS + k * 8, 8), 8)] = imag

    def first(k, carry):
        rows = pl.ds(pl.multiple_of(k * 8, 8), 8)
        save(dft16([(columns[a, 0, rows], columns[a, 1, rows]) for a in range(LEAD)], -1), k)
        return carry

    for part in range(GROUP):
        arriving[part].wait()
        lax.fori_loop(part * PART // 8, (part + 1) * PART // 8, first, 0, unroll=UNROLL)
    run_all(tables, "wait")
    mix_left(store, table_high, table_low)

    def modulus(k, carry):
        rows = pl.ds(pl.multiple_of(k * 8, 8), 8)
        residual = []
        for a, (real, imag) in enumerate(dft16([load(c, k) for c in range(LEAD)], 1)):
            share = columns[a, 2, rows] * lax.rsqrt(jnp.maximum(real * real + imag * imag, 0.0625))
            keep = 1.0 - share
            residual.append((real * keep, -imag * keep))
        save(dft16(residual, -1), k)
        return carry

    measured.wait()
    lax.fori_loop(0, ROWS // 8, modulus, 0, unroll=UNROLL)
    mix_left(store, table_high, table_low)

    def last(k, carry):
        rows = pl.ds(pl.multiple_of(k * 8, 8), 8)
        for a, (real, imag) in enumerate(dft16([load(c, k) for c in range(LEAD)], 1)):
            at = pl.multiple_of((a + 1) * ROWS + k * 8, 8)
            for half, value in enumerate((real, -imag)):
                straight[half, a, rows] = value
                wrapped[half, pl.ds(at, 8)] = value
                if a == LEAD - 1:
                    wrapped[half, rows] = value
        return carry

    sends = []

    def send(source, half, part):
        target = out.at[pl.ds(part * LEAD, LEAD), half]
        copy = pltpu.make_async_copy(source.at[half % 2, :, pieces[part]], target, out_sems.at[half, part])
        copy.start()
        sends.append(copy)

    for part in range(GROUP):
        lax.fori_loop(part * PART // 8, (part + 1) * PART // 8, last, 0, unroll=UNROLL)
        send(straight, 0, part)
        send(straight, 1, part)
    base = lax.div(shifts[0] + 7, 8) * 8
    keep = lax.broadcasted_iota(jnp.int32, (8, LANES), 0) < 8 - (base - shifts[0])
    back = lax.rem(8 - (base - shifts[0]), 8)
    limit = wrapped.shape[1] - 8

    for part in range(GROUP):

        def place(a, carry):
            start = (a + 1) * ROWS + part * PART - base
            for half in range(2):
                rolled = []
                for k in range(PART // 8 + 1):
                    at = pl.multiple_of(jnp.minimum(start + 8 * k, limit), 8)
                    rolled.append(pltpu.roll(wrapped[half, pl.ds(at, 8)], back, 0))
                for k in range(PART // 8):
                    rows = pl.ds(part * PART + 8 * k, 8)
                    shifted[half, a, rows] = jnp.where(keep, rolled[k], rolled[k + 1])
            return carry

        lax.fori_loop(0, LEAD, place, 0, unroll=UNROLL)
        send(shifted, 2, part)
        send(shifted, 3, part)
    run_all(sends, "wait")


def gradient_kernel(shifts, rows_in, *refs):
    halo = 2 + GROUP
    object_own, object_below = refs[2 + halo : 4 + halo], refs[4 + halo : 6 + halo]
    table_high, table_low, out = refs[6 + halo : 9 + halo]
    probe_window, object_window, store, probe_acc, object_acc, sems, halo_sems = refs[9 + halo :]
    core = shifts[2 * GROUP + 1]
    held = block_copies(probe_window, refs[:2], ROWS, sems.at[0])
    held += block_copies(object_window, object_own, 0, sems.at[1])
    held += block_copies(object_window, object_below, ROWS, sems.at[2])
    moved = halo_copies(probe_window, refs[2 : 2 + halo], 0, shifts, halo_sems)
    run_all(held, "start")
    run_halo(moved, core == 1, "start")
    own = shifts[2 * GROUP]
    own_start = own * PART
    chunks = PART // 8

    def first(m, carry):
        aligned = lax.div(m, GROUP * chunks)
        position = lax.rem(lax.div(m, chunks), GROUP)
        rows = pl.ds(pl.multiple_of(lax.rem(m, chunks) * 8, 8), 8)
        at = pl.ds(pl.multiple_of(m * 8, 8), 8)
        values = [
            (rows_in[position * LEAD + a, 2 * aligned, rows], -rows_in[position * LEAD + a, 2 * aligned + 1, rows])
            for a in range(LEAD)
        ]
        for c, (real, imag) in enumerate(dft16(values, -1)):
            store[c, at, pl.ds(0, LANES)] = real
            store[c, at, pl.ds(LANES, LANES)] = imag
        return carry

    lax.fori_loop(0, 2 * GROUP * chunks, first, 0, unroll=UNROLL)
    mix_right(store, table_high, table_low)
    run_all(held, "wait")
    run_halo(moved, core == 1, "wait")
    probe_acc[...] = jnp.zeros_like(probe_acc)
    object_acc[...] = jnp.zeros_like(object_acc)

    def back(m):
        at = pl.ds(pl.multiple_of(m * 8, 8), 8)
        values = [(store[c, at, pl.ds(0, LANES)], store[c, at, pl.ds(LANES, LANES)]) for c in range(LEAD)]
        return [(real, -imag) for real, imag in dft16(values, 1)]

    def probe_term(m, carry):
        position = lax.div(m, chunks)
        offset = pl.multiple_of(lax.rem(m, chunks) * 8, 8)
        rows = pl.ds(offset, 8)
        entry = 2 * lax.bitwise_xor(own, position)
        tile, shift = lane_parts(shifts[entry + 1])
        start = own_start + shifts[entry] + offset
        patch_r = shifted_tiles(object_window, 0, start, tile, shift)
        patch_i = shifted_tiles(object_window, 1, start, tile, shift)
        for a, (real, imag) in enumerate(back(m)):
            lanes = pl.ds(a * LANES, LANES)
            probe_acc[0, rows, lanes] += patch_r[a] * real + patch_i[a] * imag
            probe_acc[1, rows, lanes] += patch_r[a] * imag - patch_i[a] * real
        return carry

    lax.fori_loop(0, GROUP * chunks, probe_term, 0, unroll=UNROLL)
    lane = lax.broadcasted_iota(jnp.int32, (8, LANES), 1)

    def object_term(m, carry):
        position = lax.div(m, chunks)
        offset = pl.multiple_of(lax.rem(m, chunks) * 8, 8)
        rows = pl.ds(offset, 8)
        entry = 2 * lax.bitwise_xor(own, position)
        tile, shift = lane_parts(shifts[entry + 1])
        start = ROWS + own_start - shifts[entry] + offset
        rolled = []
        for a, (real, imag) in enumerate(back(GROUP * chunks + m)):
            lanes = pl.ds(a * LANES, LANES)
            probe_real = eight_rows(probe_window, 0, start, lanes)
            probe_imag = eight_rows(probe_window, 1, start, lanes)
            rolled.append(
                (
                    pltpu.roll(probe_real * real + probe_imag * imag, shift, 1),
                    pltpu.roll(probe_real * imag - probe_imag * real, shift, 1),
                )
            )
        keep = lane >= shift
        for j in range(LEAD + 1):
            lanes = pl.ds(pl.multiple_of((tile + j) * LANES, LANES), LANES)
            for half in range(2):
                here = rolled[j][half] if j < LEAD else 0.0
                left = rolled[j - 1][half] if j > 0 else 0.0
                object_acc[half, rows, lanes] += jnp.where(keep, here, left)
        return carry

    lax.fori_loop(0, GROUP * chunks, object_term, 0, unroll=UNROLL)
    own = object_acc.shape[2] // LANES * LANES
    width = LANES + LANES // 8
    for b in range(LEAD):
        for half in range(2):
            out[b, pl.ds(half * PART, PART)] = probe_acc[half, :, pl.ds(b * LANES, LANES)]
            out[b, pl.ds((2 + half) * PART, PART)] = object_acc[half, :, pl.ds(b * width, LANES)]
        pieces = []
        for k in range(chunks):
            for half in range(2):
                pieces.append(object_acc[half, pl.ds(8 * k, 8), pl.ds(b * width + LANES, width - LANES)])
        out[b, pl.ds(4 * PART, 8)] = jnp.concatenate(pieces, 1)


def total_kernel(terms, probe_r, probe_i, object_r, object_i):
    width = LANES // 8
    totals = []
    for part in range(GROUP):
        total = terms[part]
        for high in range(1, LEAD // GROUP):
            total = total + terms[high * GROUP + part]
        totals.append(total)
    for half, (probe_out, object_out) in enumerate(((probe_r, object_r), (probe_i, object_i))):
        for part in range(GROUP):
            probe_out[pl.ds(part * PART, PART)] = totals[part][half * PART : (half + 1) * PART]
        left = [totals[part][(2 + half) * PART : (3 + half) * PART] for part in range(GROUP)]
        object_out[pl.ds(0, LANES)] = jnp.concatenate(left, 0).T
        right = []
        for part in range(GROUP):
            for k in range(PART // 8):
                at = (2 * k + half) * width
                right.append(totals[part][4 * PART : 4 * PART + 8, at : at + width])
        object_out[pl.ds(LANES, width)] = jnp.concatenate(right, 0).T


SMEM = pl.BlockSpec(memory_space=pltpu.SMEM)
VMEM = pl.BlockSpec(memory_space=pltpu.VMEM)
ANY = pl.BlockSpec(memory_space=pl.ANY)


def params(mebibytes):
    return pltpu.CompilerParams(vmem_limit_bytes=mebibytes * MEBI)


def shape(*sizes):
    return jax.ShapeDtypeStruct(sizes, F32)


def row_pairs(by, inside):
    pairs = [(r, (r + by) % LEAD) for r in range(LEAD)]
    return [(a, b) for a, b in pairs if (a // 2 == b // 2) == inside]


def fetched_part():
    return lax.axis_index(("zh", "zl")) % GROUP


def own_part(place, real, imag):
    return pl.pallas_call(
        part_kernel,
        out_shape=shape(2, PART, real.shape[1]),
        in_specs=[SMEM, ANY, ANY],
        out_specs=VMEM,
        scratch_shapes=[pltpu.SemaphoreType.DMA((2,))],
        compiler_params=params(4),
        name="part_kernel",
    )(place, real, imag)


def passed_on(part, takers):
    parts = [part]
    for by in range(1, GROUP):
        pairs = []
        for z in range(8):
            for yl in range(2):
                if z % GROUP >= 2 * ((z ^ by) % 2) + yl:
                    pairs += [((2 * z + yl) * LEAD + r, (2 * (z ^ by) + yl) * LEAD + r) for r in takers]
        parts.append(lax.ppermute(part, ("zh", "zl", "yl", "row"), pairs))
    return tuple(parts)


def together(*values):
    return lax.optimization_barrier(values)


def per_device(tables, probe_r, probe_i, object_r, object_i, amplitudes, row_shift, col_shift):
    right_high, right_low, left_high, left_low = tables
    width = object_r.shape[1]
    field = probe_r.shape[1]
    group = ("zl", "yl")
    below_r, below_i = (
        lax.ppermute(value, "row", row_pairs(-1, False) + row_pairs(-1, True)) for value in (object_r, object_i)
    )
    own = lax.axis_index(group).astype(jnp.int32)
    core = lax.axis_index("row").astype(jnp.int32) % 2
    part = fetched_part().astype(jnp.int32)
    own_shift = jnp.concatenate([row_shift, col_shift])
    others = [
        lax.ppermute(own_shift, group, [(i, i ^ by) for i in range(GROUP)]) for by in range(1, GROUP)
    ]
    all_shifts = jnp.concatenate([own_shift] + others + [own[None], core[None], part[None]])
    above_part = own_part(part[None], probe_r, probe_i)
    near_above = tuple(lax.ppermute(value, "row", row_pairs(1, True)) for value in (probe_r, probe_i))
    below_r, below_i, above_part, all_shifts, near_above = together(
        below_r, below_i, above_part, all_shifts, near_above
    )
    above_part = lax.ppermute(above_part, "row", row_pairs(1, False))
    exit_spread = pl.pallas_call(
        exit_kernel,
        out_shape=shape(LEAD, 3, ROWS, LANES),
        in_specs=[SMEM, ANY, ANY, ANY, ANY, ANY, ANY, ANY, ANY, ANY],
        out_specs=ANY,
        scratch_shapes=[
            pltpu.VMEM((2, 2 * ROWS, width), F32),
            pltpu.VMEM((2, ROWS, field), F32),
            pltpu.VMEM(right_high.shape, BF16),
            pltpu.VMEM(right_low.shape, BF16),
            pltpu.VMEM((LEAD, ROWS, 2 * LANES), F32),
            pltpu.VMEM((LEAD, 3, ROWS, LANES), F32),
            pltpu.SemaphoreType.DMA((3 * GROUP, 2)),
            pltpu.SemaphoreType.DMA((2,)),
            pltpu.SemaphoreType.DMA((LEAD,)),
            pltpu.SemaphoreType.DMA((GROUP,)),
        ],
        compiler_params=params(60),
        cost_estimate=pl.CostEstimate(flops=int(2e9), bytes_accessed=int(20e6), transcendentals=0),
        name="exit_kernel",
    )(
        all_shifts, probe_r, probe_i, object_r, object_i, below_r, below_i, amplitudes, right_high,
        right_low,
    )
    exit_spread, above_part = together(exit_spread, above_part)
    columns = lax.all_to_all(exit_spread, "row", 0, 0, tiled=True)
    above = passed_on(above_part, range(0, LEAD, 2))
    returned = pl.pallas_call(
        detector_kernel,
        out_shape=shape(GROUP * LEAD, 4, PART, LANES),
        in_specs=[SMEM, ANY, ANY, ANY],
        out_specs=ANY,
        scratch_shapes=[
            pltpu.VMEM((LEAD, 3, ROWS, LANES), F32),
            pltpu.VMEM(left_high.shape, BF16),
            pltpu.VMEM(left_low.shape, BF16),
            pltpu.VMEM((LEAD, 2 * ROWS, LANES), F32),
            pltpu.VMEM((2, (LEAD + 1) * ROWS, LANES), F32),
            pltpu.VMEM((2, LEAD, ROWS, LANES), F32),
            pltpu.VMEM((2, LEAD, ROWS, LANES), F32),
            pltpu.SemaphoreType.DMA((GROUP,)),
            pltpu.SemaphoreType.DMA((3,)),
            pltpu.SemaphoreType.DMA((4, GROUP)),
        ],
        compiler_params=params(60),
        cost_estimate=pl.CostEstimate(flops=4000000000, bytes_accessed=36000000, transcendentals=0),
        name="detector_kernel",
    )(all_shifts, columns, left_high, left_low)
    returned, above = together(returned, above)
    rows_in = lax.all_to_all(returned, group + ("row",), 0, 0, tiled=True)
    terms = pl.pallas_call(
        gradient_kernel,
        out_shape=shape(LEAD, 4 * PART + 8, LANES),
        in_specs=[SMEM, VMEM] + [ANY] * (8 + GROUP) + [VMEM, VMEM],
        out_specs=VMEM,
        scratch_shapes=[
            pltpu.VMEM((2, 2 * ROWS, field), F32),
            pltpu.VMEM((2, 2 * ROWS, width), F32),
            pltpu.VMEM((LEAD, 2 * ROWS, 2 * LANES), F32),
            pltpu.VMEM((2, PART, field), F32),
            pltpu.VMEM((2, PART, width + LANES), F32),
            pltpu.SemaphoreType.DMA((3, 2)),
            pltpu.SemaphoreType.DMA((GROUP, 2)),
        ],
        compiler_params=params(28),
        cost_estimate=pl.CostEstimate(flops=4000000000, bytes_accessed=50000000, transcendentals=0),
        name="gradient_kernel",
    )(
        all_shifts, rows_in, probe_r, probe_i, *near_above, *above, object_r, object_i, below_r, below_i,
        right_high, right_low,
    )
    terms = lax.all_to_all(terms, ("zh",) + group, 0, 0, tiled=True)
    own_width = width // LEAD
    probe_r, probe_i, object_r, object_i = pl.pallas_call(
        total_kernel,
        out_shape=(shape(ROWS, LANES), shape(ROWS, LANES), shape(own_width, ROWS), shape(own_width, ROWS)),
        in_specs=[VMEM],
        out_specs=(VMEM, VMEM, VMEM, VMEM),
        compiler_params=params(8),
        cost_estimate=pl.CostEstimate(flops=10000000, bytes_accessed=6000000, transcendentals=0),
        name="total_kernel",
    )(terms)
    return probe_r, probe_i, object_r.T, object_i.T


def solution(mesh):
    fine = Mesh(mesh.devices.reshape(4, 2, 2, LEAD), ("zh", "zl", "yl", "row"))
    batch = ("zh", "zl", "yl")
    tables = propagation_tables(LEAD * LANES)

    def step(*arguments):
        held = tuple(jnp.asarray(table) for table in tables)
        return functools.partial(per_device, held)(*arguments)

    placed = (
        P("row", None),
        P("row", None),
        P("row", None),
        P("row", None),
        P(batch, "row", None),
        P(batch),
        P(batch),
    )
    return jax.shard_map(
        step,
        mesh=fine,
        in_specs=placed,
        out_specs=(P("row", batch),) * 4,
        check_vma=False,
    )
```

```python
import functools
import math

import jax
import jax.numpy as jnp
import ml_dtypes
import numpy as np
from jax import lax
from jax.experimental import pallas as pl
from jax.experimental.pallas import tpu as pltpu
from jax.sharding import Mesh, PartitionSpec as P

F32 = jnp.float32
BF16 = jnp.bfloat16
LANES = 128
LEAD = 16
ROWS = 128
GROUP = 4
UNROLL = 4
PART = ROWS // GROUP
MEBI = 1024 * 1024


def split_pair(table):
    high = table.astype(ml_dtypes.bfloat16)
    low = (table - high.astype(np.float64)).astype(ml_dtypes.bfloat16)
    return high, low


@functools.lru_cache(maxsize=None)
def propagation_tables(length):
    index = np.arange(length, dtype=np.int64)
    frequency = np.where(index < length // 2, index, index - length)
    chirp = np.exp(-2j * np.pi * ((frequency * frequency) % (4 * length)) / (4 * length))
    offsets = np.arange(-(LANES - 1), LANES, dtype=np.int64)
    place = np.arange(LANES)
    right, left = np.empty((LEAD, LANES, 2 * LANES)), np.empty((LEAD, LANES, 2 * LANES))
    for c in range(LEAD):
        tone = c + LEAD * np.arange(LANES, dtype=np.int64)
        phase = np.exp(2j * np.pi * ((offsets[:, None] * tone[None, :]) % length) / length)
        line = phase @ chirp[tone] / length
        middle = line[place[:, None] - place[None, :] + LANES - 1]
        right[c] = np.concatenate([middle.real.T, middle.imag.T], 1)
        left[c] = np.concatenate([middle.real, middle.imag], 1)
    return split_pair(right) + split_pair(left)


def times(value, cosine, sine):
    real, imag = value
    if sine == 0.0 and cosine == 1.0:
        return value
    if cosine == 0.0 and sine == -1.0:
        return (imag, -real)
    if cosine == 0.0 and sine == 1.0:
        return (-imag, real)
    return (real * cosine - imag * sine, real * sine + imag * cosine)


def add(left, right):
    return (left[0] + right[0], left[1] + right[1])


def sub(left, right):
    return (left[0] - right[0], left[1] - right[1])


def dft4(values, sign):
    a, b, c, d = values
    even, odd = add(a, c), sub(a, c)
    both, gap = add(b, d), sub(b, d)
    turned = (-sign * gap[1], sign * gap[0]) if sign < 0 else (-gap[1], gap[0])
    if sign < 0:
        turned = (gap[1], -gap[0])
    return [add(even, both), add(odd, turned), sub(even, both), sub(odd, turned)]


def dft16(values, sign):
    inner = [dft4([values[4 * n1 + n2] for n1 in range(4)], sign) for n2 in range(4)]
    result = [None] * 16
    for k1 in range(4):
        column = []
        for n2 in range(4):
            turns = n2 * k1 % 16
            angle = 2.0 * math.pi * turns / 16
            cosine, sine = math.cos(angle), sign * math.sin(angle)
            if turns in (0, 4, 8, 12):
                cosine, sine = float(round(cosine)), float(round(sine))
            column.append(times(inner[n2][k1], cosine, sine))
        for k2, value in enumerate(dft4(column, sign)):
            result[k1 + 4 * k2] = value
    return result


def halves(value):
    high = value.astype(BF16)
    return high, (value - high.astype(F32)).astype(BF16)


def dot(left, right):
    return jnp.dot(left, right, preferred_element_type=F32)


def right_block(pair):
    real, imag = pair[:, :LANES], pair[:, LANES:]
    return jnp.concatenate([pair, jnp.concatenate([-imag, real], 1)], 0)


def left_block(pair):
    real, imag = pair[:, :LANES], pair[:, LANES:]
    return jnp.concatenate([jnp.concatenate([real, -imag], 1), jnp.concatenate([imag, real], 1)], 0)


def mix_right(store, table_high, table_low):
    rows = store.shape[1]

    def step(c, carry):
        high, low = halves(store[c])
        wide = dot(jnp.concatenate([high, low], 0), right_block(table_high[c]))
        store[c] = wide[:rows] + (wide[rows:] + dot(high, right_block(table_low[c])))
        return carry

    lax.fori_loop(0, LEAD, step, 0, unroll=True)


def mix_left(store, table_high, table_low):
    cols = store.shape[2]

    def step(c, carry):
        high, low = halves(store[c])
        wide = dot(left_block(table_high[c]), jnp.concatenate([high, low], 1))
        store[c] = wide[:, :cols] + (wide[:, cols:] + dot(left_block(table_low[c]), high))
        return carry

    lax.fori_loop(0, LEAD, step, 0, unroll=True)


def lane_parts(col_shift):
    tile = lax.div(col_shift, LANES)
    return tile, col_shift - tile * LANES


def eight_rows(window, part, start, lanes):
    base = lax.div(start, 8) * 8
    shift = start - base
    after = jnp.minimum(base + 8, window.shape[1] - 8)
    back = lax.rem(8 - shift, 8)
    upper = pltpu.roll(window[part, pl.ds(pl.multiple_of(base, 8), 8), lanes], back, 0)
    lower = pltpu.roll(window[part, pl.ds(pl.multiple_of(after, 8), 8), lanes], back, 0)
    row = lax.broadcasted_iota(jnp.int32, upper.shape, 0)
    return jnp.where(row < 8 - shift, upper, lower)


def shifted_tiles(window, part, row_start, tile, shift):
    last = window.shape[2] // LANES - 1
    back = lax.rem(LANES - shift, LANES)
    lane = lax.broadcasted_iota(jnp.int32, (8, LANES), 1)
    rolled = []
    for j in range(LEAD + 1):
        at = pl.multiple_of(jnp.minimum(tile + j, last) * LANES, LANES)
        rolled.append(pltpu.roll(eight_rows(window, part, row_start, pl.ds(at, LANES)), back, 1))
    keep = lane < LANES - shift
    return [jnp.where(keep, rolled[j], rolled[j + 1]) for j in range(LEAD)]


def block_copies(window, block, at, sems):
    rows = block[0].shape[0]
    return [
        pltpu.make_async_copy(block[half], window.at[half, pl.ds(at, rows)], sems.at[half])
        for half in range(2)
    ]


def halo_copies(window, halo, at, shifts, sems):
    near = block_copies(window, halo[:2], at, sems.at[0])
    far = []
    for by in range(GROUP):
        part = halo[2 + by]
        place = pl.multiple_of(at + PART * lax.bitwise_xor(shifts[2 * GROUP + 2], by), PART)
        far += block_copies(window, (part.at[0], part.at[1]), place, sems.at[by])
    return near, far


def run_all(copies, method):
    for copy in copies:
        getattr(copy, method)()


def run_halo(copies, from_chip, method):
    @pl.when(from_chip)
    def _():
        run_all(copies[0], method)

    @pl.when(jnp.logical_not(from_chip))
    def _():
        run_all(copies[1], method)


def part_kernel(place, real, imag, out, sems):
    rows = pl.ds(pl.multiple_of(place[0] * PART, PART), PART)
    copies = block_copies(out, (real.at[rows], imag.at[rows]), 0, sems)
    run_all(copies, "start")
    run_all(copies, "wait")


def exit_kernel(
    shifts, probe_r, probe_i, object_r, object_i, below_r, below_i, high_in, low_in, out,
    window, probe, table_high, table_low, store, spread, sems, table_sems, out_sems,
):
    row_shift = shifts[0]
    held, moved, pieces = [], [], []
    for part in range(GROUP):
        rows = pl.ds(part * PART, PART)
        held.append(block_copies(window, (object_r.at[rows], object_i.at[rows]), part * PART, sems.at[part]))
        moved.append(
            block_copies(window, (below_r.at[rows], below_i.at[rows]), ROWS + part * PART, sems.at[GROUP + part])
        )
        pieces.append(
            block_copies(probe, (probe_r.at[rows], probe_i.at[rows]), part * PART, sems.at[2 * GROUP + part])
        )

    def run_held(part, method):
        @pl.when(row_shift < (part + 1) * PART)
        def _():
            run_all(held[part], method)

    def run_moved(part, method):
        @pl.when(row_shift > part * PART)
        def _():
            run_all(moved[part], method)

    tables = [
        pltpu.make_async_copy(source, target, table_sems.at[n])
        for n, (source, target) in enumerate(((high_in, table_high), (low_in, table_low)))
    ]
    for part in range(GROUP):
        run_held(part, "start")
    for part in range(GROUP):
        run_moved(part, "start")
        run_all(pieces[part], "start")
    run_all(tables, "start")
    for part in range(GROUP):
        run_held(part, "wait")
    tile, shift = lane_parts(shifts[1])

    def gather(k, carry):
        at = pl.multiple_of(k * 8, 8)
        rows = pl.ds(at, 8)
        patch_r = shifted_tiles(window, 0, row_shift + at, tile, shift)
        patch_i = shifted_tiles(window, 1, row_shift + at, tile, shift)
        values = []
        for a in range(LEAD):
            lanes = pl.ds(a * LANES, LANES)
            real, imag = probe[0, rows, lanes], probe[1, rows, lanes]
            values.append(
                (real * patch_r[a] - imag * patch_i[a], real * patch_i[a] + imag * patch_r[a])
            )
        for c, (real, imag) in enumerate(dft16(values, -1)):
            store[c, rows, pl.ds(0, LANES)] = real
            store[c, rows, pl.ds(LANES, LANES)] = imag
        return carry

    for part in range(GROUP):
        run_moved(part, "wait")
        run_all(pieces[part], "wait")
        lax.fori_loop(part * PART // 8, (part + 1) * PART // 8, gather, 0, unroll=UNROLL)
    run_all(tables, "wait")
    mix_right(store, table_high, table_low)

    def scatter(k, carry):
        rows = pl.ds(pl.multiple_of(k * 8, 8), 8)
        values = [(store[c, rows, pl.ds(0, LANES)], store[c, rows, pl.ds(LANES, LANES)]) for c in range(LEAD)]
        for a, (real, imag) in enumerate(dft16(values, 1)):
            spread[a, 0, rows] = real
            spread[a, 1, rows] = imag
        return carry

    sends = []
    for part in range(GROUP):
        lax.fori_loop(part * PART // 8, (part + 1) * PART // 8, scatter, 0, unroll=UNROLL)
        rows = pl.ds(part * PART, PART)
        send = pltpu.make_async_copy(spread.at[:, :, rows], out.at[:, :, rows], out_sems.at[part])
        send.start()
        sends.append(send)
    run_all(sends, "wait")


def detector_kernel(
    shifts, columns_in, measured_in, high_in, low_in, out, columns, measured, table_high, table_low, store,
    wrapped, straight, shifted, sems, table_sems, out_sems,
):
    pieces = [pl.ds(part * PART, PART) for part in range(GROUP)]
    arriving = [
        pltpu.make_async_copy(columns_in.at[:, :, rows], columns.at[:, :, rows], sems.at[part])
        for part, rows in enumerate(pieces)
    ]
    tables = [
        pltpu.make_async_copy(source, target, table_sems.at[n])
        for n, (source, target) in enumerate(((high_in, table_high), (low_in, table_low)))
    ]
    amplitudes = pltpu.make_async_copy(measured_in, measured, table_sems.at[2])
    run_all(arriving, "start")
    run_all(tables, "start")
    amplitudes.start()

    def load(c, k):
        at = pl.multiple_of(k * 8, 8)
        return (store[c, pl.ds(at, 8)], store[c, pl.ds(pl.multiple_of(ROWS + k * 8, 8), 8)])

    def save(values, k):
        for c, (real, imag) in enumerate(values):
            store[c, pl.ds(pl.multiple_of(k * 8, 8), 8)] = real
            store[c, pl.ds(pl.multiple_of(ROWS + k * 8, 8), 8)] = imag

    def first(k, carry):
        rows = pl.ds(pl.multiple_of(k * 8, 8), 8)
        save(dft16([(columns[a, 0, rows], columns[a, 1, rows]) for a in range(LEAD)], -1), k)
        return carry

    for part in range(GROUP):
        arriving[part].wait()
        lax.fori_loop(part * PART // 8, (part + 1) * PART // 8, first, 0, unroll=UNROLL)
    run_all(tables, "wait")
    mix_left(store, table_high, table_low)

    def modulus(k, carry):
        rows = pl.ds(pl.multiple_of(k * 8, 8), 8)
        residual = []
        for a, (real, imag) in enumerate(dft16([load(c, k) for c in range(LEAD)], 1)):
            share = measured[a, rows] * lax.rsqrt(jnp.maximum(real * real + imag * imag, 0.0625))
            keep = 1.0 - share
            residual.append((real * keep, -imag * keep))
        save(dft16(residual, -1), k)
        return carry

    amplitudes.wait()
    lax.fori_loop(0, ROWS // 8, modulus, 0, unroll=UNROLL)
    mix_left(store, table_high, table_low)

    def last(k, carry):
        rows = pl.ds(pl.multiple_of(k * 8, 8), 8)
        for a, (real, imag) in enumerate(dft16([load(c, k) for c in range(LEAD)], 1)):
            at = pl.multiple_of((a + 1) * ROWS + k * 8, 8)
            for half, value in enumerate((real, -imag)):
                straight[half, a, rows] = value
                wrapped[half, pl.ds(at, 8)] = value
                if a == LEAD - 1:
                    wrapped[half, rows] = value
        return carry

    sends = []

    def send(source, half, part):
        target = out.at[pl.ds(part * LEAD, LEAD), half]
        copy = pltpu.make_async_copy(source.at[half % 2, :, pieces[part]], target, out_sems.at[half, part])
        copy.start()
        sends.append(copy)

    for part in range(GROUP):
        lax.fori_loop(part * PART // 8, (part + 1) * PART // 8, last, 0, unroll=UNROLL)
        send(straight, 0, part)
        send(straight, 1, part)
    base = lax.div(shifts[0] + 7, 8) * 8
    keep = lax.broadcasted_iota(jnp.int32, (8, LANES), 0) < 8 - (base - shifts[0])
    back = lax.rem(8 - (base - shifts[0]), 8)
    limit = wrapped.shape[1] - 8

    for part in range(GROUP):

        def place(a, carry):
            start = (a + 1) * ROWS + part * PART - base
            for half in range(2):
                rolled = []
                for k in range(PART // 8 + 1):
                    at = pl.multiple_of(jnp.minimum(start + 8 * k, limit), 8)
                    rolled.append(pltpu.roll(wrapped[half, pl.ds(at, 8)], back, 0))
                for k in range(PART // 8):
                    rows = pl.ds(part * PART + 8 * k, 8)
                    shifted[half, a, rows] = jnp.where(keep, rolled[k], rolled[k + 1])
            return carry

        lax.fori_loop(0, LEAD, place, 0, unroll=UNROLL)
        send(shifted, 2, part)
        send(shifted, 3, part)
    run_all(sends, "wait")


def gradient_kernel(shifts, rows_in, *refs):
    halo = 2 + GROUP
    object_own, object_below = refs[2 + halo : 4 + halo], refs[4 + halo : 6 + halo]
    table_high, table_low, out = refs[6 + halo : 9 + halo]
    probe_window, object_window, store, probe_acc, object_acc, sems, halo_sems = refs[9 + halo :]
    core = shifts[2 * GROUP + 1]
    held = block_copies(probe_window, refs[:2], ROWS, sems.at[0])
    held += block_copies(object_window, object_own, 0, sems.at[1])
    held += block_copies(object_window, object_below, ROWS, sems.at[2])
    moved = halo_copies(probe_window, refs[2 : 2 + halo], 0, shifts, halo_sems)
    run_all(held, "start")
    run_halo(moved, core == 1, "start")
    own = shifts[2 * GROUP]
    own_start = own * PART
    chunks = PART // 8

    def first(m, carry):
        aligned = lax.div(m, GROUP * chunks)
        position = lax.rem(lax.div(m, chunks), GROUP)
        rows = pl.ds(pl.multiple_of(lax.rem(m, chunks) * 8, 8), 8)
        at = pl.ds(pl.multiple_of(m * 8, 8), 8)
        values = [
            (rows_in[position * LEAD + a, 2 * aligned, rows], -rows_in[position * LEAD + a, 2 * aligned + 1, rows])
            for a in range(LEAD)
        ]
        for c, (real, imag) in enumerate(dft16(values, -1)):
            store[c, at, pl.ds(0, LANES)] = real
            store[c, at, pl.ds(LANES, LANES)] = imag
        return carry

    lax.fori_loop(0, 2 * GROUP * chunks, first, 0, unroll=UNROLL)
    mix_right(store, table_high, table_low)
    run_all(held, "wait")
    run_halo(moved, core == 1, "wait")
    probe_acc[...] = jnp.zeros_like(probe_acc)
    object_acc[...] = jnp.zeros_like(object_acc)

    def back(m):
        at = pl.ds(pl.multiple_of(m * 8, 8), 8)
        values = [(store[c, at, pl.ds(0, LANES)], store[c, at, pl.ds(LANES, LANES)]) for c in range(LEAD)]
        return [(real, -imag) for real, imag in dft16(values, 1)]

    def probe_term(m, carry):
        position = lax.div(m, chunks)
        offset = pl.multiple_of(lax.rem(m, chunks) * 8, 8)
        rows = pl.ds(offset, 8)
        entry = 2 * lax.bitwise_xor(own, position)
        tile, shift = lane_parts(shifts[entry + 1])
        start = own_start + shifts[entry] + offset
        patch_r = shifted_tiles(object_window, 0, start, tile, shift)
        patch_i = shifted_tiles(object_window, 1, start, tile, shift)
        for a, (real, imag) in enumerate(back(m)):
            lanes = pl.ds(a * LANES, LANES)
            probe_acc[0, rows, lanes] += patch_r[a] * real + patch_i[a] * imag
            probe_acc[1, rows, lanes] += patch_r[a] * imag - patch_i[a] * real
        return carry

    lax.fori_loop(0, GROUP * chunks, probe_term, 0, unroll=UNROLL)
    lane = lax.broadcasted_iota(jnp.int32, (8, LANES), 1)

    def object_term(m, carry):
        position = lax.div(m, chunks)
        offset = pl.multiple_of(lax.rem(m, chunks) * 8, 8)
        rows = pl.ds(offset, 8)
        entry = 2 * lax.bitwise_xor(own, position)
        tile, shift = lane_parts(shifts[entry + 1])
        start = ROWS + own_start - shifts[entry] + offset
        rolled = []
        for a, (real, imag) in enumerate(back(GROUP * chunks + m)):
            lanes = pl.ds(a * LANES, LANES)
            probe_real = eight_rows(probe_window, 0, start, lanes)
            probe_imag = eight_rows(probe_window, 1, start, lanes)
            rolled.append(
                (
                    pltpu.roll(probe_real * real + probe_imag * imag, shift, 1),
                    pltpu.roll(probe_real * imag - probe_imag * real, shift, 1),
                )
            )
        keep = lane >= shift
        for j in range(LEAD + 1):
            lanes = pl.ds(pl.multiple_of((tile + j) * LANES, LANES), LANES)
            for half in range(2):
                here = rolled[j][half] if j < LEAD else 0.0
                left = rolled[j - 1][half] if j > 0 else 0.0
                object_acc[half, rows, lanes] += jnp.where(keep, here, left)
        return carry

    lax.fori_loop(0, GROUP * chunks, object_term, 0, unroll=UNROLL)
    own = object_acc.shape[2] // LANES * LANES
    width = LANES + LANES // 8
    for b in range(LEAD):
        for half in range(2):
            out[b, pl.ds(half * PART, PART)] = probe_acc[half, :, pl.ds(b * LANES, LANES)]
            out[b, pl.ds((2 + half) * PART, PART)] = object_acc[half, :, pl.ds(b * width, LANES)]
        pieces = []
        for k in range(chunks):
            for half in range(2):
                pieces.append(object_acc[half, pl.ds(8 * k, 8), pl.ds(b * width + LANES, width - LANES)])
        out[b, pl.ds(4 * PART, 8)] = jnp.concatenate(pieces, 1)


def total_kernel(terms, probe_r, probe_i, object_r, object_i):
    width = LANES // 8
    totals = []
    for part in range(GROUP):
        total = terms[part]
        for high in range(1, LEAD // GROUP):
            total = total + terms[high * GROUP + part]
        totals.append(total)
    for half, (probe_out, object_out) in enumerate(((probe_r, object_r), (probe_i, object_i))):
        for part in range(GROUP):
            probe_out[pl.ds(part * PART, PART)] = totals[part][half * PART : (half + 1) * PART]
        left = [totals[part][(2 + half) * PART : (3 + half) * PART] for part in range(GROUP)]
        object_out[pl.ds(0, LANES)] = jnp.concatenate(left, 0).T
        right = []
        for part in range(GROUP):
            for k in range(PART // 8):
                at = (2 * k + half) * width
                right.append(totals[part][4 * PART : 4 * PART + 8, at : at + width])
        object_out[pl.ds(LANES, width)] = jnp.concatenate(right, 0).T


SMEM = pl.BlockSpec(memory_space=pltpu.SMEM)
VMEM = pl.BlockSpec(memory_space=pltpu.VMEM)
ANY = pl.BlockSpec(memory_space=pl.ANY)


def params(mebibytes):
    return pltpu.CompilerParams(vmem_limit_bytes=mebibytes * MEBI)


def shape(*sizes):
    return jax.ShapeDtypeStruct(sizes, F32)


def row_pairs(by, inside):
    pairs = [(r, (r + by) % LEAD) for r in range(LEAD)]
    return [(a, b) for a, b in pairs if (a // 2 == b // 2) == inside]


def fetched_part():
    return lax.axis_index(("zh", "zl")) % GROUP


def own_part(place, real, imag):
    return pl.pallas_call(
        part_kernel,
        out_shape=shape(2, PART, real.shape[1]),
        in_specs=[SMEM, ANY, ANY],
        out_specs=VMEM,
        scratch_shapes=[pltpu.SemaphoreType.DMA((2,))],
        compiler_params=params(4),
        name="part_kernel",
    )(place, real, imag)


def passed_on(part, takers):
    parts = [part]
    for by in range(1, GROUP):
        pairs = []
        for z in range(8):
            for yl in range(2):
                if z % GROUP >= 2 * ((z ^ by) % 2) + yl:
                    pairs += [((2 * z + yl) * LEAD + r, (2 * (z ^ by) + yl) * LEAD + r) for r in takers]
        parts.append(lax.ppermute(part, ("zh", "zl", "yl", "row"), pairs))
    return tuple(parts)


def together(*values):
    return lax.optimization_barrier(values)


def per_device(tables, probe_r, probe_i, object_r, object_i, amplitudes, row_shift, col_shift):
    right_high, right_low, left_high, left_low = tables
    width = object_r.shape[1]
    field = probe_r.shape[1]
    group = ("zl", "yl")
    below_r, below_i = (
        lax.ppermute(value, "row", row_pairs(-1, False) + row_pairs(-1, True)) for value in (object_r, object_i)
    )
    own = lax.axis_index(group).astype(jnp.int32)
    core = lax.axis_index("row").astype(jnp.int32) % 2
    part = fetched_part().astype(jnp.int32)
    own_shift = jnp.concatenate([row_shift, col_shift])
    measured = amplitudes[0].reshape(ROWS, LEAD, LANES).transpose(1, 0, 2)
    measured = lax.all_to_all(measured, "row", 0, 0, tiled=True)
    above_part = own_part(part[None], probe_r, probe_i)
    near_above = tuple(lax.ppermute(value, "row", row_pairs(1, True)) for value in (probe_r, probe_i))
    below_r, below_i, above_part, near_above = together(below_r, below_i, above_part, near_above)
    above_part = lax.ppermute(above_part, "row", row_pairs(1, False))
    exit_spread = pl.pallas_call(
        exit_kernel,
        out_shape=shape(LEAD, 2, ROWS, LANES),
        in_specs=[SMEM] + [ANY] * 8,
        out_specs=ANY,
        scratch_shapes=[
            pltpu.VMEM((2, 2 * ROWS, width), F32),
            pltpu.VMEM((2, ROWS, field), F32),
            pltpu.VMEM(right_high.shape, BF16),
            pltpu.VMEM(right_low.shape, BF16),
            pltpu.VMEM((LEAD, ROWS, 2 * LANES), F32),
            pltpu.VMEM((LEAD, 2, ROWS, LANES), F32),
            pltpu.SemaphoreType.DMA((3 * GROUP, 2)),
            pltpu.SemaphoreType.DMA((2,)),
            pltpu.SemaphoreType.DMA((GROUP,)),
        ],
        compiler_params=params(60),
        name="exit_kernel",
    )(
        own_shift, probe_r, probe_i, object_r, object_i, below_r, below_i, right_high, right_low,
    )
    exit_spread, above_part, measured, late_shift = together(
        exit_spread, above_part, measured, own_shift
    )
    columns = lax.all_to_all(exit_spread, "row", 0, 0, tiled=True)
    others = [
        lax.ppermute(late_shift, group, [(i, i ^ by) for i in range(GROUP)]) for by in range(1, GROUP)
    ]
    all_shifts = jnp.concatenate([late_shift] + others + [own[None], core[None], part[None]])
    above = passed_on(above_part, range(0, LEAD, 2))
    returned = pl.pallas_call(
        detector_kernel,
        out_shape=shape(GROUP * LEAD, 4, PART, LANES),
        in_specs=[SMEM, ANY, ANY, ANY, ANY],
        out_specs=ANY,
        scratch_shapes=[
            pltpu.VMEM((LEAD, 2, ROWS, LANES), F32),
            pltpu.VMEM((LEAD, ROWS, LANES), F32),
            pltpu.VMEM(left_high.shape, BF16),
            pltpu.VMEM(left_low.shape, BF16),
            pltpu.VMEM((LEAD, 2 * ROWS, LANES), F32),
            pltpu.VMEM((2, (LEAD + 1) * ROWS, LANES), F32),
            pltpu.VMEM((2, LEAD, ROWS, LANES), F32),
            pltpu.VMEM((2, LEAD, ROWS, LANES), F32),
            pltpu.SemaphoreType.DMA((GROUP,)),
            pltpu.SemaphoreType.DMA((3,)),
            pltpu.SemaphoreType.DMA((4, GROUP)),
        ],
        compiler_params=params(60),
        cost_estimate=pl.CostEstimate(flops=4000000000, bytes_accessed=36000000, transcendentals=0),
        name="detector_kernel",
    )(own_shift, columns, measured, left_high, left_low)
    returned, above, all_shifts = together(returned, above, all_shifts)
    rows_in = lax.all_to_all(returned, group + ("row",), 0, 0, tiled=True)
    terms = pl.pallas_call(
        gradient_kernel,
        out_shape=shape(LEAD, 4 * PART + 8, LANES),
        in_specs=[SMEM, VMEM] + [ANY] * (8 + GROUP) + [VMEM, VMEM],
        out_specs=VMEM,
        scratch_shapes=[
            pltpu.VMEM((2, 2 * ROWS, field), F32),
            pltpu.VMEM((2, 2 * ROWS, width), F32),
            pltpu.VMEM((LEAD, 2 * ROWS, 2 * LANES), F32),
            pltpu.VMEM((2, PART, field), F32),
            pltpu.VMEM((2, PART, width + LANES), F32),
            pltpu.SemaphoreType.DMA((3, 2)),
            pltpu.SemaphoreType.DMA((GROUP, 2)),
        ],
        compiler_params=params(28),
        cost_estimate=pl.CostEstimate(flops=4000000000, bytes_accessed=50000000, transcendentals=0),
        name="gradient_kernel",
    )(
        all_shifts, rows_in, probe_r, probe_i, *near_above, *above, object_r, object_i, below_r, below_i,
        right_high, right_low,
    )
    terms = lax.all_to_all(terms, ("zh",) + group, 0, 0, tiled=True)
    own_width = width // LEAD
    probe_r, probe_i, object_r, object_i = pl.pallas_call(
        total_kernel,
        out_shape=(shape(ROWS, LANES), shape(ROWS, LANES), shape(own_width, ROWS), shape(own_width, ROWS)),
        in_specs=[VMEM],
        out_specs=(VMEM, VMEM, VMEM, VMEM),
        compiler_params=params(8),
        cost_estimate=pl.CostEstimate(flops=10000000, bytes_accessed=6000000, transcendentals=0),
        name="total_kernel",
    )(terms)
    return probe_r, probe_i, object_r.T, object_i.T


def solution(mesh):
    fine = Mesh(mesh.devices.reshape(4, 2, 2, LEAD), ("zh", "zl", "yl", "row"))
    batch = ("zh", "zl", "yl")
    tables = propagation_tables(LEAD * LANES)

    def step(*arguments):
        held = tuple(jnp.asarray(table) for table in tables)
        return functools.partial(per_device, held)(*arguments)

    placed = (
        P("row", None),
        P("row", None),
        P("row", None),
        P("row", None),
        P(batch, "row", None),
        P(batch),
        P(batch),
    )
    return jax.shard_map(
        step,
        mesh=fine,
        in_specs=placed,
        out_specs=(P("row", batch),) * 4,
        check_vma=False,
    )
```

```python
import functools
import math

import jax
import jax.numpy as jnp
import ml_dtypes
import numpy as np
from jax import lax
from jax.experimental import pallas as pl
from jax.experimental.pallas import tpu as pltpu
from jax.sharding import Mesh, PartitionSpec as P

F32 = jnp.float32
BF16 = jnp.bfloat16
LANES = 128
LEAD = 16
ROWS = 128
GROUP = 4
UNROLL = 4
PART = ROWS // GROUP
MEBI = 1024 * 1024


def split_pair(table):
    high = table.astype(ml_dtypes.bfloat16)
    low = (table - high.astype(np.float64)).astype(ml_dtypes.bfloat16)
    return high, low


@functools.lru_cache(maxsize=None)
def propagation_tables(length):
    index = np.arange(length, dtype=np.int64)
    frequency = np.where(index < length // 2, index, index - length)
    chirp = np.exp(-2j * np.pi * ((frequency * frequency) % (4 * length)) / (4 * length))
    offsets = np.arange(-(LANES - 1), LANES, dtype=np.int64)
    place = np.arange(LANES)
    right, left = np.empty((LEAD, LANES, 2 * LANES)), np.empty((LEAD, LANES, 2 * LANES))
    for c in range(LEAD):
        tone = c + LEAD * np.arange(LANES, dtype=np.int64)
        phase = np.exp(2j * np.pi * ((offsets[:, None] * tone[None, :]) % length) / length)
        line = phase @ chirp[tone] / length
        middle = line[place[:, None] - place[None, :] + LANES - 1]
        right[c] = np.concatenate([middle.real.T, middle.imag.T], 1)
        left[c] = np.concatenate([middle.real, middle.imag], 1)
    return split_pair(right) + split_pair(left)


def times(value, cosine, sine):
    real, imag = value
    if sine == 0.0 and cosine == 1.0:
        return value
    if cosine == 0.0 and sine == -1.0:
        return (imag, -real)
    if cosine == 0.0 and sine == 1.0:
        return (-imag, real)
    return (real * cosine - imag * sine, real * sine + imag * cosine)


def add(left, right):
    return (left[0] + right[0], left[1] + right[1])


def sub(left, right):
    return (left[0] - right[0], left[1] - right[1])


def dft4(values, sign):
    a, b, c, d = values
    even, odd = add(a, c), sub(a, c)
    both, gap = add(b, d), sub(b, d)
    turned = (-sign * gap[1], sign * gap[0]) if sign < 0 else (-gap[1], gap[0])
    if sign < 0:
        turned = (gap[1], -gap[0])
    return [add(even, both), add(odd, turned), sub(even, both), sub(odd, turned)]


def dft16(values, sign):
    inner = [dft4([values[4 * n1 + n2] for n1 in range(4)], sign) for n2 in range(4)]
    result = [None] * 16
    for k1 in range(4):
        column = []
        for n2 in range(4):
            turns = n2 * k1 % 16
            angle = 2.0 * math.pi * turns / 16
            cosine, sine = math.cos(angle), sign * math.sin(angle)
            if turns in (0, 4, 8, 12):
                cosine, sine = float(round(cosine)), float(round(sine))
            column.append(times(inner[n2][k1], cosine, sine))
        for k2, value in enumerate(dft4(column, sign)):
            result[k1 + 4 * k2] = value
    return result


def halves(value):
    high = value.astype(BF16)
    return high, (value - high.astype(F32)).astype(BF16)


def dot(left, right):
    return jnp.dot(left, right, preferred_element_type=F32)


def right_block(pair):
    real, imag = pair[:, :LANES], pair[:, LANES:]
    return jnp.concatenate([pair, jnp.concatenate([-imag, real], 1)], 0)


def left_block(pair):
    real, imag = pair[:, :LANES], pair[:, LANES:]
    return jnp.concatenate([jnp.concatenate([real, -imag], 1), jnp.concatenate([imag, real], 1)], 0)


def mix_right(store, table_high, table_low):
    rows = store.shape[1]

    def step(c, carry):
        high, low = halves(store[c])
        wide = dot(jnp.concatenate([high, low], 0), right_block(table_high[c]))
        store[c] = wide[:rows] + (wide[rows:] + dot(high, right_block(table_low[c])))
        return carry

    lax.fori_loop(0, LEAD, step, 0, unroll=True)


def mix_left(store, table_high, table_low):
    cols = store.shape[2]

    def step(c, carry):
        high, low = halves(store[c])
        wide = dot(left_block(table_high[c]), jnp.concatenate([high, low], 1))
        store[c] = wide[:, :cols] + (wide[:, cols:] + dot(left_block(table_low[c]), high))
        return carry

    lax.fori_loop(0, LEAD, step, 0, unroll=True)


def lane_parts(col_shift):
    tile = lax.div(col_shift, LANES)
    return tile, col_shift - tile * LANES


def eight_rows(window, part, start, lanes):
    base = lax.div(start, 8) * 8
    shift = start - base
    after = jnp.minimum(base + 8, window.shape[1] - 8)
    back = lax.rem(8 - shift, 8)
    upper = pltpu.roll(window[part, pl.ds(pl.multiple_of(base, 8), 8), lanes], back, 0)
    lower = pltpu.roll(window[part, pl.ds(pl.multiple_of(after, 8), 8), lanes], back, 0)
    row = lax.broadcasted_iota(jnp.int32, upper.shape, 0)
    return jnp.where(row < 8 - shift, upper, lower)


def shifted_tiles(window, part, row_start, tile, shift):
    last = window.shape[2] // LANES - 1
    back = lax.rem(LANES - shift, LANES)
    lane = lax.broadcasted_iota(jnp.int32, (8, LANES), 1)
    rolled = []
    for j in range(LEAD + 1):
        at = pl.multiple_of(jnp.minimum(tile + j, last) * LANES, LANES)
        rolled.append(pltpu.roll(eight_rows(window, part, row_start, pl.ds(at, LANES)), back, 1))
    keep = lane < LANES - shift
    return [jnp.where(keep, rolled[j], rolled[j + 1]) for j in range(LEAD)]


def block_copies(window, block, at, sems):
    rows = block[0].shape[0]
    return [
        pltpu.make_async_copy(block[half], window.at[half, pl.ds(at, rows)], sems.at[half])
        for half in range(2)
    ]


def halo_copies(window, halo, at, shifts, sems):
    near = block_copies(window, halo[:2], at, sems.at[0])
    far = []
    for by in range(GROUP):
        part = halo[2 + by]
        place = pl.multiple_of(at + PART * lax.bitwise_xor(shifts[2 * GROUP + 2], by), PART)
        far += block_copies(window, (part.at[0], part.at[1]), place, sems.at[by])
    return near, far


def run_all(copies, method):
    for copy in copies:
        getattr(copy, method)()


def run_halo(copies, from_chip, method):
    @pl.when(from_chip)
    def _():
        run_all(copies[0], method)

    @pl.when(jnp.logical_not(from_chip))
    def _():
        run_all(copies[1], method)


def part_kernel(place, real, imag, out, sems):
    rows = pl.ds(pl.multiple_of(place[0] * PART, PART), PART)
    copies = block_copies(out, (real.at[rows], imag.at[rows]), 0, sems)
    run_all(copies, "start")
    run_all(copies, "wait")


def exit_kernel(
    shifts, probe_r, probe_i, object_r, object_i, below_r, below_i, high_in, low_in, out,
    window, probe, table_high, table_low, store, spread, sems, table_sems, out_sems,
):
    row_shift = shifts[0]
    held, moved, pieces = [], [], []
    for part in range(GROUP):
        rows = pl.ds(part * PART, PART)
        held.append(block_copies(window, (object_r.at[rows], object_i.at[rows]), part * PART, sems.at[part]))
        moved.append(
            block_copies(window, (below_r.at[rows], below_i.at[rows]), ROWS + part * PART, sems.at[GROUP + part])
        )
        pieces.append(
            block_copies(probe, (probe_r.at[rows], probe_i.at[rows]), part * PART, sems.at[2 * GROUP + part])
        )

    def run_held(part, method):
        @pl.when(row_shift < (part + 1) * PART)
        def _():
            run_all(held[part], method)

    def run_moved(part, method):
        @pl.when(row_shift > part * PART)
        def _():
            run_all(moved[part], method)

    tables = [
        pltpu.make_async_copy(source, target, table_sems.at[n])
        for n, (source, target) in enumerate(((high_in, table_high), (low_in, table_low)))
    ]
    for part in range(GROUP):
        run_held(part, "start")
    for part in range(GROUP):
        run_moved(part, "start")
        run_all(pieces[part], "start")
    run_all(tables, "start")
    for part in range(GROUP):
        run_held(part, "wait")
    tile, shift = lane_parts(shifts[1])

    def gather(k, carry):
        at = pl.multiple_of(k * 8, 8)
        rows = pl.ds(at, 8)
        patch_r = shifted_tiles(window, 0, row_shift + at, tile, shift)
        patch_i = shifted_tiles(window, 1, row_shift + at, tile, shift)
        values = []
        for a in range(LEAD):
            lanes = pl.ds(a * LANES, LANES)
            real, imag = probe[0, rows, lanes], probe[1, rows, lanes]
            values.append(
                (real * patch_r[a] - imag * patch_i[a], real * patch_i[a] + imag * patch_r[a])
            )
        for c, (real, imag) in enumerate(dft16(values, -1)):
            store[c, rows, pl.ds(0, LANES)] = real
            store[c, rows, pl.ds(LANES, LANES)] = imag
        return carry

    for part in range(GROUP):
        run_moved(part, "wait")
        run_all(pieces[part], "wait")
        lax.fori_loop(part * PART // 8, (part + 1) * PART // 8, gather, 0, unroll=UNROLL)
    run_all(tables, "wait")
    mix_right(store, table_high, table_low)

    def scatter(k, carry):
        rows = pl.ds(pl.multiple_of(k * 8, 8), 8)
        values = [(store[c, rows, pl.ds(0, LANES)], store[c, rows, pl.ds(LANES, LANES)]) for c in range(LEAD)]
        for a, (real, imag) in enumerate(dft16(values, 1)):
            spread[a, 0, rows] = real
            spread[a, 1, rows] = imag
        return carry

    sends = []
    for part in range(GROUP):
        lax.fori_loop(part * PART // 8, (part + 1) * PART // 8, scatter, 0, unroll=UNROLL)
        rows = pl.ds(part * PART, PART)
        send = pltpu.make_async_copy(spread.at[:, :, rows], out.at[:, :, rows], out_sems.at[part])
        send.start()
        sends.append(send)
    run_all(sends, "wait")


def detector_kernel(
    shifts, columns_in, measured_in, high_in, low_in, out, columns, measured, table_high, table_low, store,
    wrapped, straight, shifted, sems, table_sems, out_sems,
):
    pieces = [pl.ds(part * PART, PART) for part in range(GROUP)]
    arriving = [
        pltpu.make_async_copy(columns_in.at[:, :, rows], columns.at[:, :, rows], sems.at[part])
        for part, rows in enumerate(pieces)
    ]
    tables = [
        pltpu.make_async_copy(source, target, table_sems.at[n])
        for n, (source, target) in enumerate(((high_in, table_high), (low_in, table_low)))
    ]
    amplitudes = pltpu.make_async_copy(measured_in, measured, table_sems.at[2])
    run_all(arriving, "start")
    run_all(tables, "start")
    amplitudes.start()

    def load(c, k):
        at = pl.multiple_of(k * 8, 8)
        return (store[c, pl.ds(at, 8)], store[c, pl.ds(pl.multiple_of(ROWS + k * 8, 8), 8)])

    def save(values, k):
        for c, (real, imag) in enumerate(values):
            store[c, pl.ds(pl.multiple_of(k * 8, 8), 8)] = real
            store[c, pl.ds(pl.multiple_of(ROWS + k * 8, 8), 8)] = imag

    def first(k, carry):
        rows = pl.ds(pl.multiple_of(k * 8, 8), 8)
        save(dft16([(columns[a, 0, rows], columns[a, 1, rows]) for a in range(LEAD)], -1), k)
        return carry

    for part in range(GROUP):
        arriving[part].wait()
        lax.fori_loop(part * PART // 8, (part + 1) * PART // 8, first, 0, unroll=UNROLL)
    run_all(tables, "wait")
    mix_left(store, table_high, table_low)

    def modulus(k, carry):
        rows = pl.ds(pl.multiple_of(k * 8, 8), 8)
        residual = []
        for a, (real, imag) in enumerate(dft16([load(c, k) for c in range(LEAD)], 1)):
            share = measured[a, rows] * lax.rsqrt(jnp.maximum(real * real + imag * imag, 0.0625))
            keep = 1.0 - share
            residual.append((real * keep, -imag * keep))
        save(dft16(residual, -1), k)
        return carry

    amplitudes.wait()
    lax.fori_loop(0, ROWS // 8, modulus, 0, unroll=UNROLL)
    mix_left(store, table_high, table_low)

    def last(k, carry):
        rows = pl.ds(pl.multiple_of(k * 8, 8), 8)
        for a, (real, imag) in enumerate(dft16([load(c, k) for c in range(LEAD)], 1)):
            at = pl.multiple_of((a + 1) * ROWS + k * 8, 8)
            for half, value in enumerate((real, -imag)):
                straight[half, a, rows] = value
                wrapped[half, pl.ds(at, 8)] = value
                if a == LEAD - 1:
                    wrapped[half, rows] = value
        return carry

    sends = []

    def send(source, half, part):
        target = out.at[pl.ds(part * LEAD, LEAD), half]
        copy = pltpu.make_async_copy(source.at[half % 2, :, pieces[part]], target, out_sems.at[half, part])
        copy.start()
        sends.append(copy)

    for part in range(GROUP):
        lax.fori_loop(part * PART // 8, (part + 1) * PART // 8, last, 0, unroll=UNROLL)
        send(straight, 0, part)
        send(straight, 1, part)
    base = lax.div(shifts[0] + 7, 8) * 8
    keep = lax.broadcasted_iota(jnp.int32, (8, LANES), 0) < 8 - (base - shifts[0])
    back = lax.rem(8 - (base - shifts[0]), 8)
    limit = wrapped.shape[1] - 8

    for part in range(GROUP):

        def place(a, carry):
            start = (a + 1) * ROWS + part * PART - base
            for half in range(2):
                rolled = []
                for k in range(PART // 8 + 1):
                    at = pl.multiple_of(jnp.minimum(start + 8 * k, limit), 8)
                    rolled.append(pltpu.roll(wrapped[half, pl.ds(at, 8)], back, 0))
                for k in range(PART // 8):
                    rows = pl.ds(part * PART + 8 * k, 8)
                    shifted[half, a, rows] = jnp.where(keep, rolled[k], rolled[k + 1])
            return carry

        lax.fori_loop(0, LEAD, place, 0, unroll=UNROLL)
        send(shifted, 2, part)
        send(shifted, 3, part)
    run_all(sends, "wait")


def gradient_kernel(shifts, rows_in, *refs):
    halo = 2 + GROUP
    object_own, object_below = refs[2 + halo : 4 + halo], refs[4 + halo : 6 + halo]
    table_high, table_low, out = refs[6 + halo : 9 + halo]
    probe_window, object_window, store, probe_acc, object_acc, sems, halo_sems = refs[9 + halo :]
    core = shifts[2 * GROUP + 1]
    held = block_copies(probe_window, refs[:2], ROWS, sems.at[0])
    held += block_copies(object_window, object_own, 0, sems.at[1])
    held += block_copies(object_window, object_below, ROWS, sems.at[2])
    moved = halo_copies(probe_window, refs[2 : 2 + halo], 0, shifts, halo_sems)
    run_all(held, "start")
    run_halo(moved, core == 1, "start")
    own = shifts[2 * GROUP]
    own_start = own * PART
    chunks = PART // 8

    def first(m, carry):
        aligned = lax.div(m, GROUP * chunks)
        position = lax.rem(lax.div(m, chunks), GROUP)
        rows = pl.ds(pl.multiple_of(lax.rem(m, chunks) * 8, 8), 8)
        at = pl.ds(pl.multiple_of(m * 8, 8), 8)
        values = [
            (rows_in[position * LEAD + a, 2 * aligned, rows], -rows_in[position * LEAD + a, 2 * aligned + 1, rows])
            for a in range(LEAD)
        ]
        for c, (real, imag) in enumerate(dft16(values, -1)):
            store[c, at, pl.ds(0, LANES)] = real
            store[c, at, pl.ds(LANES, LANES)] = imag
        return carry

    lax.fori_loop(0, 2 * GROUP * chunks, first, 0, unroll=UNROLL)
    mix_right(store, table_high, table_low)
    run_all(held, "wait")
    run_halo(moved, core == 1, "wait")
    probe_acc[...] = jnp.zeros_like(probe_acc)
    object_acc[...] = jnp.zeros_like(object_acc)

    def back(m):
        at = pl.ds(pl.multiple_of(m * 8, 8), 8)
        values = [(store[c, at, pl.ds(0, LANES)], store[c, at, pl.ds(LANES, LANES)]) for c in range(LEAD)]
        return [(real, -imag) for real, imag in dft16(values, 1)]

    def probe_term(m, carry):
        position = lax.div(m, chunks)
        offset = pl.multiple_of(lax.rem(m, chunks) * 8, 8)
        rows = pl.ds(offset, 8)
        entry = 2 * lax.bitwise_xor(own, position)
        tile, shift = lane_parts(shifts[entry + 1])
        start = own_start + shifts[entry] + offset
        patch_r = shifted_tiles(object_window, 0, start, tile, shift)
        patch_i = shifted_tiles(object_window, 1, start, tile, shift)
        for a, (real, imag) in enumerate(back(m)):
            lanes = pl.ds(a * LANES, LANES)
            probe_acc[0, rows, lanes] += patch_r[a] * real + patch_i[a] * imag
            probe_acc[1, rows, lanes] += patch_r[a] * imag - patch_i[a] * real
        return carry

    lax.fori_loop(0, GROUP * chunks, probe_term, 0, unroll=UNROLL)
    lane = lax.broadcasted_iota(jnp.int32, (8, LANES), 1)

    def object_term(m, carry):
        position = lax.div(m, chunks)
        offset = pl.multiple_of(lax.rem(m, chunks) * 8, 8)
        rows = pl.ds(offset, 8)
        entry = 2 * lax.bitwise_xor(own, position)
        tile, shift = lane_parts(shifts[entry + 1])
        start = ROWS + own_start - shifts[entry] + offset
        rolled = []
        for a, (real, imag) in enumerate(back(GROUP * chunks + m)):
            lanes = pl.ds(a * LANES, LANES)
            probe_real = eight_rows(probe_window, 0, start, lanes)
            probe_imag = eight_rows(probe_window, 1, start, lanes)
            rolled.append(
                (
                    pltpu.roll(probe_real * real + probe_imag * imag, shift, 1),
                    pltpu.roll(probe_real * imag - probe_imag * real, shift, 1),
                )
            )
        keep = lane >= shift
        for j in range(LEAD + 1):
            lanes = pl.ds(pl.multiple_of((tile + j) * LANES, LANES), LANES)
            for half in range(2):
                here = rolled[j][half] if j < LEAD else 0.0
                left = rolled[j - 1][half] if j > 0 else 0.0
                object_acc[half, rows, lanes] += jnp.where(keep, here, left)
        return carry

    lax.fori_loop(0, GROUP * chunks, object_term, 0, unroll=UNROLL)
    own = object_acc.shape[2] // LANES * LANES
    width = LANES + LANES // 8
    for b in range(LEAD):
        for half in range(2):
            out[b, pl.ds(half * PART, PART)] = probe_acc[half, :, pl.ds(b * LANES, LANES)]
            out[b, pl.ds((2 + half) * PART, PART)] = object_acc[half, :, pl.ds(b * width, LANES)]
        pieces = []
        for k in range(chunks):
            for half in range(2):
                pieces.append(object_acc[half, pl.ds(8 * k, 8), pl.ds(b * width + LANES, width - LANES)])
        out[b, pl.ds(4 * PART, 8)] = jnp.concatenate(pieces, 1)


def total_kernel(terms, probe_r, probe_i, object_r, object_i):
    width = LANES // 8
    totals = []
    for part in range(GROUP):
        total = terms[part]
        for high in range(1, LEAD // GROUP):
            total = total + terms[high * GROUP + part]
        totals.append(total)
    for half, (probe_out, object_out) in enumerate(((probe_r, object_r), (probe_i, object_i))):
        for part in range(GROUP):
            probe_out[pl.ds(part * PART, PART)] = totals[part][half * PART : (half + 1) * PART]
        left = [totals[part][(2 + half) * PART : (3 + half) * PART] for part in range(GROUP)]
        object_out[pl.ds(0, LANES)] = jnp.concatenate(left, 0).T
        right = []
        for part in range(GROUP):
            for k in range(PART // 8):
                at = (2 * k + half) * width
                right.append(totals[part][4 * PART : 4 * PART + 8, at : at + width])
        object_out[pl.ds(LANES, width)] = jnp.concatenate(right, 0).T


SMEM = pl.BlockSpec(memory_space=pltpu.SMEM)
VMEM = pl.BlockSpec(memory_space=pltpu.VMEM)
ANY = pl.BlockSpec(memory_space=pl.ANY)


def params(mebibytes):
    return pltpu.CompilerParams(vmem_limit_bytes=mebibytes * MEBI)


def shape(*sizes):
    return jax.ShapeDtypeStruct(sizes, F32)


def row_pairs(by, inside):
    pairs = [(r, (r + by) % LEAD) for r in range(LEAD)]
    return [(a, b) for a, b in pairs if (a // 2 == b // 2) == inside]


def fetched_part():
    return lax.axis_index(("zh", "zl")) % GROUP


def own_part(place, real, imag):
    return pl.pallas_call(
        part_kernel,
        out_shape=shape(2, PART, real.shape[1]),
        in_specs=[SMEM, ANY, ANY],
        out_specs=VMEM,
        scratch_shapes=[pltpu.SemaphoreType.DMA((2,))],
        compiler_params=params(4),
        name="part_kernel",
    )(place, real, imag)


def passed_on(part, takers):
    parts = [part]
    for by in range(1, GROUP):
        pairs = []
        for z in range(8):
            for yl in range(2):
                if z % GROUP >= 2 * ((z ^ by) % 2) + yl:
                    pairs += [((2 * z + yl) * LEAD + r, (2 * (z ^ by) + yl) * LEAD + r) for r in takers]
        parts.append(lax.ppermute(part, ("zh", "zl", "yl", "row"), pairs))
    return tuple(parts)


def together(*values):
    return lax.optimization_barrier(values)


def per_device(tables, probe_r, probe_i, object_r, object_i, amplitudes, row_shift, col_shift):
    right_high, right_low, left_high, left_low = tables
    width = object_r.shape[1]
    field = probe_r.shape[1]
    group = ("zl", "yl")
    below_r, below_i = (
        lax.ppermute(value, "row", row_pairs(-1, False) + row_pairs(-1, True)) for value in (object_r, object_i)
    )
    own = lax.axis_index(group).astype(jnp.int32)
    core = lax.axis_index("row").astype(jnp.int32) % 2
    part = fetched_part().astype(jnp.int32)
    own_shift = jnp.concatenate([row_shift, col_shift])
    measured = amplitudes[0].reshape(ROWS, LEAD, LANES).transpose(1, 0, 2)
    measured = lax.all_to_all(measured, "row", 0, 0, tiled=True)
    above_part = own_part(part[None], probe_r, probe_i)
    near_above = tuple(lax.ppermute(value, "row", row_pairs(1, True)) for value in (probe_r, probe_i))
    below_r, below_i, above_part, near_above, own_shift = together(
        below_r, below_i, above_part, near_above, own_shift
    )
    above_part = lax.ppermute(above_part, "row", row_pairs(1, False))
    exit_spread = pl.pallas_call(
        exit_kernel,
        out_shape=shape(LEAD, 2, ROWS, LANES),
        in_specs=[SMEM] + [ANY] * 8,
        out_specs=ANY,
        scratch_shapes=[
            pltpu.VMEM((2, 2 * ROWS, width), F32),
            pltpu.VMEM((2, ROWS, field), F32),
            pltpu.VMEM(right_high.shape, BF16),
            pltpu.VMEM(right_low.shape, BF16),
            pltpu.VMEM((LEAD, ROWS, 2 * LANES), F32),
            pltpu.VMEM((LEAD, 2, ROWS, LANES), F32),
            pltpu.SemaphoreType.DMA((3 * GROUP, 2)),
            pltpu.SemaphoreType.DMA((2,)),
            pltpu.SemaphoreType.DMA((GROUP,)),
        ],
        compiler_params=params(60),
        name="exit_kernel",
    )(
        own_shift, probe_r, probe_i, object_r, object_i, below_r, below_i, right_high, right_low,
    )
    exit_spread, above_part, measured, late_shift = together(
        exit_spread, above_part, measured, own_shift
    )
    columns = lax.all_to_all(exit_spread, "row", 0, 0, tiled=True)
    others = [
        lax.ppermute(late_shift, group, [(i, i ^ by) for i in range(GROUP)]) for by in range(1, GROUP)
    ]
    all_shifts = jnp.concatenate([late_shift] + others + [own[None], core[None], part[None]])
    above = passed_on(above_part, range(0, LEAD, 2))
    returned = pl.pallas_call(
        detector_kernel,
        out_shape=shape(GROUP * LEAD, 4, PART, LANES),
        in_specs=[SMEM, ANY, ANY, ANY, ANY],
        out_specs=ANY,
        scratch_shapes=[
            pltpu.VMEM((LEAD, 2, ROWS, LANES), F32),
            pltpu.VMEM((LEAD, ROWS, LANES), F32),
            pltpu.VMEM(left_high.shape, BF16),
            pltpu.VMEM(left_low.shape, BF16),
            pltpu.VMEM((LEAD, 2 * ROWS, LANES), F32),
            pltpu.VMEM((2, (LEAD + 1) * ROWS, LANES), F32),
            pltpu.VMEM((2, LEAD, ROWS, LANES), F32),
            pltpu.VMEM((2, LEAD, ROWS, LANES), F32),
            pltpu.SemaphoreType.DMA((GROUP,)),
            pltpu.SemaphoreType.DMA((3,)),
            pltpu.SemaphoreType.DMA((4, GROUP)),
        ],
        compiler_params=params(60),
        cost_estimate=pl.CostEstimate(flops=4000000000, bytes_accessed=36000000, transcendentals=0),
        name="detector_kernel",
    )(own_shift, columns, measured, left_high, left_low)
    returned, above, all_shifts = together(returned, above, all_shifts)
    rows_in = lax.all_to_all(returned, group + ("row",), 0, 0, tiled=True)
    terms = pl.pallas_call(
        gradient_kernel,
        out_shape=shape(LEAD, 4 * PART + 8, LANES),
        in_specs=[SMEM, VMEM] + [ANY] * (8 + GROUP) + [VMEM, VMEM],
        out_specs=VMEM,
        scratch_shapes=[
            pltpu.VMEM((2, 2 * ROWS, field), F32),
            pltpu.VMEM((2, 2 * ROWS, width), F32),
            pltpu.VMEM((LEAD, 2 * ROWS, 2 * LANES), F32),
            pltpu.VMEM((2, PART, field), F32),
            pltpu.VMEM((2, PART, width + LANES), F32),
            pltpu.SemaphoreType.DMA((3, 2)),
            pltpu.SemaphoreType.DMA((GROUP, 2)),
        ],
        compiler_params=params(28),
        cost_estimate=pl.CostEstimate(flops=4000000000, bytes_accessed=50000000, transcendentals=0),
        name="gradient_kernel",
    )(
        all_shifts, rows_in, probe_r, probe_i, *near_above, *above, object_r, object_i, below_r, below_i,
        right_high, right_low,
    )
    terms = lax.all_to_all(terms, ("zh",) + group, 0, 0, tiled=True)
    own_width = width // LEAD
    probe_r, probe_i, object_r, object_i = pl.pallas_call(
        total_kernel,
        out_shape=(shape(ROWS, LANES), shape(ROWS, LANES), shape(own_width, ROWS), shape(own_width, ROWS)),
        in_specs=[VMEM],
        out_specs=(VMEM, VMEM, VMEM, VMEM),
        compiler_params=params(8),
        cost_estimate=pl.CostEstimate(flops=10000000, bytes_accessed=6000000, transcendentals=0),
        name="total_kernel",
    )(terms)
    return probe_r, probe_i, object_r.T, object_i.T


def solution(mesh):
    fine = Mesh(mesh.devices.reshape(4, 2, 2, LEAD), ("zh", "zl", "yl", "row"))
    batch = ("zh", "zl", "yl")
    tables = propagation_tables(LEAD * LANES)

    def step(*arguments):
        held = tuple(jnp.asarray(table) for table in tables)
        return functools.partial(per_device, held)(*arguments)

    placed = (
        P("row", None),
        P("row", None),
        P("row", None),
        P("row", None),
        P(batch, "row", None),
        P(batch),
        P(batch),
    )
    return jax.shard_map(
        step,
        mesh=fine,
        in_specs=placed,
        out_specs=(P("row", batch),) * 4,
        check_vma=False,
    )
```
